32 devices in a mesh: groups: 2 (over x), leaf: 16 (over z, y, core).
Axes of the slice: x: 2, y: 2, z: 4, core: 2. Of those that a mesh axis runs over, the one named last changes fastest.
Arguments:
- right_sides: float32 [16, 131072], P(None, ('groups', 'leaf')), parts along dimension 1, may hold values from -6 to 6
- point_coords: float32 [3, 131072], P(None, ('groups', 'leaf')), parts along dimension 1, may hold values from 0 to 3
- cluster_order: int32 [131072], P(('groups', 'leaf')), parts along dimension 0, may hold values from 0 to 4095, as said below
- leaf_basis: float32 [32, 131072], P(None, ('groups', 'leaf')), parts along dimension 1, may hold values from -0.75 to 0.75
- child_transfer: float32 [1024, 2048], P(('groups', 'leaf')), parts along dimension 0, may hold values from -0.75 to 0.75
- root_transfer: float32 [1024, 1024], P(('groups', 'leaf')), parts along dimension 0, may hold values from -0.1875 to 0.1875
- leaf_skeleton: float32 [3, 65536], P(None, ('groups', 'leaf')), parts along dimension 1, may hold values from 0 to 3
- parent_skeleton: float32 [3, 32768], P(None, ('groups', 'leaf')), parts along dimension 1, may hold values from 0 to 3
- root_skeleton: float32 [3, 1024], P(None, ('groups', 'leaf')), parts along dimension 1, may hold values from 0 to 3
- near_pairs: int32 [2, 24576], P(None, ('groups', 'leaf')), parts along dimension 1, may hold values from 0 to 63
- near_count: int32 [32], P(('groups', 'leaf')), parts along dimension 0, may hold values from 96 to 768, as said below
- leaf_send: int32 [32, 16, 2], P(('groups', 'leaf')), parts along dimension 0, may hold values from -1 to 63, as said below
- leaf_receive: int32 [32, 16, 2], P(('groups', 'leaf')), parts along dimension 0, may hold values from -1 to 63, as said below
- parent_send: int32 [32, 16, 2], P(('groups', 'leaf')), parts along dimension 0, may hold values from -1 to 31, as said below
- parent_receive: int32 [32, 16, 2], P(('groups', 'leaf')), parts along dimension 0, may hold values from -1 to 31, as said below
- leaf_pairs: int32 [2, 8192], P(None, ('groups', 'leaf')), parts along dimension 1, may hold values from 0 to 63
- parent_pairs: int32 [2, 4096], P(None, ('groups', 'leaf')), parts along dimension 1, may hold values from 0 to 31
- top_pairs: int32 [2, 256], P(None, ('groups', 'leaf')), parts along dimension 1, may hold values from 0 to 15
Outputs:
- product: float32 [16, 131072], P(None, ('groups', 'leaf')), parts along dimension 1
The draws below stay inside these ranges and needn't reach their ends.
There are 2 independent parts, one for each index of `groups`. The reference program is written for one: setup_inputs(seed, part) draws one part's arguments, and reference() takes and returns one part's arrays. A program takes and returns all parts, laid end to end along the dimension named above; each array names one. Nothing has to cross between parts.
Inputs may be any that keep to these rules, and one draw needn't show every extreme that they name: `cluster_order`: each device's block of 4096 entries is a permutation of 0 to 4095. `near_count`: some device uses all 768 slots; near pairs past a device's count are not used. `leaf_send`: in every [p, d] the filled slots come first, their number equals that of leaf_receive[d, p]; no device sends to itself; every device receives all 2 slots from some device. `leaf_receive`: filled exactly where the matching leaf_send slot is filled. `parent_send`: as leaf_send, for level-one nodes. `parent_receive`: filled exactly where the matching parent_send slot is filled.
All inputs are finite; a program needn't handle non-finite values.
Results may differ from the reference program's by a relative error of at most 0.0003.
Values sent between devices are 32-bit elements; how exact they have to be, the bound alone decides.
A program may use at most 128 MiB of HBM per device.

```python
import jax
import jax.numpy as jnp
from jax import lax

LEAF = 64
RANK = 32
NRHS = 16
LEAVES_DEV = 64
CAP = 2
TOP_DEV = 8
P_DEV = 4096
NODES1_DEV = 32
NEAR_CAP = 768
LOCAL0 = 256
LOCAL1 = 128
POINTS = 65536
LEAVES = 1024
NODES1 = 512
N_LEAF = 16


def plan_counts(key, salt):
    key = jax.random.fold_in(key, salt)
    first_key, second_key = jax.random.split(key)
    counts = jax.random.randint(first_key, (N_LEAF, N_LEAF), 1, CAP + 1)
    offsets = jax.random.randint(second_key, (N_LEAF,), 1, N_LEAF)
    full_from = (jnp.arange(N_LEAF) + offsets) % N_LEAF
    counts = jnp.where(jnp.arange(N_LEAF)[None, :] == full_from[:, None], CAP, counts)
    counts = jnp.where(jnp.eye(N_LEAF, dtype=bool), 0, counts)
    return counts


def draw_order_helper(key, salt, node_count, counts, flip):
    key = jax.random.fold_in(key, salt)
    chosen = jax.random.randint(key, (N_LEAF, N_LEAF, CAP), 0, node_count)
    slot_ids = jnp.arange(CAP)[None, None, :]
    limits = jnp.transpose(counts) if flip else counts
    return jnp.where(slot_ids < limits[:, :, None], chosen, -1).astype(jnp.int32)


def draw_cluster_order(key, part):
    key = jax.random.fold_in(key, 11)
    block_keys = jax.random.split(key, N_LEAF)
    blocks = jax.vmap(lambda one_key: jax.random.permutation(one_key, P_DEV))(block_keys)
    return blocks.reshape(-1).astype(jnp.int32)


def draw_near_count(key, part):
    key = jax.random.fold_in(key, 12)
    first_key, second_key = jax.random.split(key)
    level_draw = jax.random.randint(first_key, (N_LEAF,), 0, 8)
    lowest = NEAR_CAP // 8
    counts = lowest + (NEAR_CAP - lowest) * level_draw * level_draw // 49
    busiest = jax.random.randint(second_key, (), 0, N_LEAF)
    return jnp.where(jnp.arange(N_LEAF) == busiest, NEAR_CAP, counts).astype(jnp.int32)


def draw_leaf_send(key, part):
    counts = plan_counts(key, 21)
    return draw_order_helper(key, 31, LEAVES_DEV, counts, True)


def draw_leaf_receive(key, part):
    counts = plan_counts(key, 21)
    return draw_order_helper(key, 41, LEAVES_DEV, counts, False)


def draw_parent_send(key, part):
    counts = plan_counts(key, 22)
    return draw_order_helper(key, 32, NODES1_DEV, counts, True)


def draw_parent_receive(key, part):
    counts = plan_counts(key, 22)
    return draw_order_helper(key, 42, NODES1_DEV, counts, False)


def place_ends(entries, own_key, low, largest):
    longest = entries.shape.index(max(entries.shape))
    spots = []
    for shift in (0, 1):
        where = [jax.random.randint(jax.random.fold_in(own_key, axis), (), 0, length) for axis, length in enumerate(entries.shape)]
        where[longest] = (where[longest] + shift) % entries.shape[longest]
        spots.append(tuple(where))
    return entries.at[spots[0]].set(low).at[spots[1]].set(largest)


def shard_levels(rng, extent, pieces, low, top_value):
    loudness, own = 1.0, jax.random.fold_in(rng, 6)
    for axis_at, blocks in pieces:
        steps = jnp.exp(jax.random.uniform(jax.random.fold_in(own, axis_at), (blocks,), jnp.float32, low / len(pieces), top_value / len(pieces)))
        loudness = loudness * jnp.repeat(steps, extent[axis_at] // blocks).reshape([-1 if axis == axis_at else 1 for axis in range(len(extent))])
    return loudness


def normal_values(stream_key, dims, scale, reach, pieces=(), held_as=jnp.bfloat16):
    gain = shard_levels(stream_key, dims, pieces, -0.22, 0.18) if pieces else 1.0
    array = jax.random.normal(stream_key, dims, jnp.float32) * scale * gain
    return jnp.minimum(jnp.maximum(array, -reach), reach).astype(held_as)


def setup_inputs(seed: int = 0, part: int = 0) -> dict:
    seeds = jax.random.split(jax.random.key(seed), 19)
    own_keys = jax.random.split(jax.random.fold_in(seeds[18], part), 19)
    return {
        "right_sides": normal_values(own_keys[0], (NRHS, POINTS), 1.0, 6.0, ((1, 16),), jnp.float32),
        "point_coords": jnp.clip(3.0 * jax.random.uniform(own_keys[1], (3, POINTS), jnp.float32) ** shard_levels(own_keys[1], (3, POINTS), ((1, 16),), -0.2, 0.2), 0.0, 3.0),
        "cluster_order": draw_cluster_order(jax.random.fold_in(jax.random.fold_in(seeds[18], part), 71), part),
        "leaf_basis": normal_values(own_keys[3], (RANK, POINTS), LEAF ** -0.5, 0.75, ((1, 16),), jnp.float32),
        "child_transfer": normal_values(own_keys[4], (NODES1, 2 * RANK * RANK), (2 * RANK) ** -0.5, 0.75, ((0, 16),), jnp.float32),
        "root_transfer": normal_values(own_keys[5], (NODES1, RANK * RANK), (NODES1_DEV * RANK) ** -0.5, 0.1875, ((0, 16),), jnp.float32),
        "leaf_skeleton": jnp.clip(3.0 * jax.random.uniform(own_keys[6], (3, LEAVES * RANK), jnp.float32) ** shard_levels(own_keys[6], (3, LEAVES * RANK), ((1, 16),), -0.2, 0.2), 0.0, 3.0),
        "parent_skeleton": jnp.clip(3.0 * jax.random.uniform(own_keys[7], (3, NODES1 * RANK), jnp.float32) ** shard_levels(own_keys[7], (3, NODES1 * RANK), ((1, 16),), -0.2, 0.2), 0.0, 3.0),
        "root_skeleton": jnp.clip(3.0 * jax.random.uniform(own_keys[8], (3, N_LEAF * RANK), jnp.float32) ** shard_levels(own_keys[8], (3, N_LEAF * RANK), ((1, 16),), -0.2, 0.2), 0.0, 3.0),
        "near_pairs": place_ends(jax.random.randint(own_keys[9], (2, N_LEAF * NEAR_CAP), 0, LEAVES_DEV), jax.random.fold_in(own_keys[9], 1), 0, LEAVES_DEV - 1).astype(jnp.int32),
        "near_count": draw_near_count(jax.random.fold_in(jax.random.fold_in(seeds[18], part), 71), part),
        "leaf_send": draw_leaf_send(jax.random.fold_in(jax.random.fold_in(seeds[18], part), 71), part),
        "leaf_receive": draw_leaf_receive(jax.random.fold_in(jax.random.fold_in(seeds[18], part), 71), part),
        "parent_send": draw_parent_send(jax.random.fold_in(jax.random.fold_in(seeds[18], part), 71), part),
        "parent_receive": draw_parent_receive(jax.random.fold_in(jax.random.fold_in(seeds[18], part), 71), part),
        "leaf_pairs": place_ends(jax.random.randint(own_keys[15], (2, N_LEAF * LOCAL0), 0, LEAVES_DEV), jax.random.fold_in(own_keys[15], 1), 0, LEAVES_DEV - 1).astype(jnp.int32),
        "parent_pairs": place_ends(jax.random.randint(own_keys[16], (2, N_LEAF * LOCAL1), 0, NODES1_DEV), jax.random.fold_in(own_keys[16], 1), 0, NODES1_DEV - 1).astype(jnp.int32),
        "top_pairs": place_ends(jax.random.randint(own_keys[17], (2, N_LEAF * TOP_DEV), 0, N_LEAF), jax.random.fold_in(own_keys[17], 1), 0, N_LEAF - 1).astype(jnp.int32),
    }


precise = lax.Precision.HIGHEST


def kernel_block(left_points, right_points):
    spacing = left_points[..., :, :, None] - right_points[..., :, None, :]
    return jnp.exp(-0.5 * jnp.sum(spacing * spacing, axis=-3))


def couple(target_points, source_points, source_moments):
    matrix = kernel_block(target_points, source_points)
    shaped = source_moments.reshape(source_moments.shape[0], RANK, NRHS)
    result = jnp.einsum("mab,mbk->mak", matrix, shaped, precision=precise)
    return result.reshape(result.shape[0], RANK * NRHS)


def near_field(leaf_points, leaf_values, pairs, used_count, block_total, block_size):
    leaf_total = leaf_points.shape[0]

    def add_block(block_index, running_total):
        block_start = block_index * block_size
        targets = lax.dynamic_slice_in_dim(pairs[0], block_start, block_size)
        sources = lax.dynamic_slice_in_dim(pairs[1], block_start, block_size)
        matrix = kernel_block(leaf_points[targets], leaf_points[sources])
        picked = leaf_values[:, sources, :]
        partial_terms = jnp.einsum("nij,knj->nki", matrix, picked, precision=precise).reshape(block_size, -1)
        is_live = (block_start + jnp.arange(block_size)) < used_count
        hits = ((targets[:, None] == jnp.arange(leaf_total)[None, :]) & is_live[:, None]).astype(jnp.float32)
        return running_total + jnp.einsum("nl,nf->lf", hits, partial_terms, precision=precise)

    start_total = jnp.zeros((leaf_total, leaf_values.shape[0] * leaf_values.shape[2]), jnp.float32)
    summed = lax.fori_loop(0, block_total, add_block, start_total)
    return summed.reshape(leaf_total, leaf_values.shape[0], leaf_values.shape[2])


def far_level(moments, skeleton, send_list, receive_list, pair_list, per_device):
    node_count = moments.shape[0]
    node_points = skeleton.reshape(3, node_count, RANK).transpose(1, 0, 2)
    pair_width = pair_list.shape[1] // N_LEAF
    owner_ids = (jnp.arange(pair_list.shape[1]) // pair_width).astype(jnp.int32)
    target_ids = (owner_ids * per_device + pair_list[0]).astype(jnp.int32)
    source_ids = (owner_ids * per_device + pair_list[1]).astype(jnp.int32)
    local_terms = couple(node_points[target_ids], node_points[source_ids], moments[source_ids])
    running_total = jax.ops.segment_sum(local_terms, target_ids, num_segments=node_count)
    sent_lists = jnp.transpose(send_list, (1, 0, 2))
    peer_ids = jnp.arange(N_LEAF, dtype=jnp.int32)[None, :, None]
    device_ids = jnp.arange(N_LEAF, dtype=jnp.int32)[:, None, None]
    is_live = (receive_list >= 0).reshape(N_LEAF, -1)
    far_sources = (peer_ids * per_device + jnp.maximum(sent_lists, 0)).astype(jnp.int32).reshape(N_LEAF, -1)
    far_targets = (device_ids * per_device + jnp.maximum(receive_list, 0)).astype(jnp.int32).reshape(N_LEAF, -1)

    def one_device(item):
        source_row, target_row, live_row = item
        partial_terms = couple(node_points[target_row], node_points[source_row], moments[source_row])
        return jnp.where(live_row[:, None], partial_terms, 0.0)

    remote_terms = lax.map(one_device, (far_sources, far_targets, is_live))
    remote_sum = jax.ops.segment_sum(remote_terms.reshape(-1, RANK * NRHS), far_targets.reshape(-1), num_segments=node_count)
    return running_total + remote_sum


def reference(right_sides, point_coords, cluster_order, leaf_basis, child_transfer, root_transfer, leaf_skeleton, parent_skeleton, root_skeleton, near_pairs, near_count, leaf_send, leaf_receive, parent_send, parent_receive, leaf_pairs, parent_pairs, top_pairs):
    owner_ids = (jnp.arange(N_LEAF * P_DEV) // P_DEV).astype(jnp.int32)
    perm = (owner_ids * P_DEV + cluster_order).astype(jnp.int32)
    ordered = right_sides[:, perm]
    sorted_points = point_coords[:, perm]
    leaf_total = N_LEAF * LEAVES_DEV
    parent_total = leaf_total // 2
    basis_blocks = leaf_basis.reshape(RANK, leaf_total, LEAF)
    leaf_moments = jnp.einsum("rlp,klp->lrk", basis_blocks, ordered.reshape(NRHS, leaf_total, LEAF), precision=precise)
    child_blocks = child_transfer.reshape(parent_total, 2, RANK, RANK)
    parent_moments = jnp.einsum("mjar,mjak->mrk", child_blocks, leaf_moments.reshape(parent_total, 2, RANK, NRHS), precision=precise)
    root_blocks = root_transfer.reshape(N_LEAF, NODES1_DEV, RANK, RANK)
    root_moments = jnp.einsum("dmar,dmak->drk", root_blocks, parent_moments.reshape(N_LEAF, NODES1_DEV, RANK, NRHS), precision=precise)
    root_points = root_skeleton.reshape(3, N_LEAF, RANK).transpose(1, 0, 2)
    top_terms = couple(root_points[top_pairs[0]], root_points[top_pairs[1]], root_moments.reshape(N_LEAF, -1)[top_pairs[1]])
    root_field = jax.ops.segment_sum(top_terms, top_pairs[0], num_segments=N_LEAF)
    parent_far = far_level(parent_moments.reshape(parent_total, -1), parent_skeleton, parent_send, parent_receive, parent_pairs, NODES1_DEV)
    leaf_far = far_level(leaf_moments.reshape(leaf_total, -1), leaf_skeleton, leaf_send, leaf_receive, leaf_pairs, LEAVES_DEV)
    parent_field = jnp.einsum("dmar,drk->dmak", root_blocks, root_field.reshape(N_LEAF, RANK, NRHS), precision=precise).reshape(parent_total, RANK * NRHS) + parent_far
    leaf_field = jnp.einsum("mjar,mrk->mjak", child_blocks, parent_field.reshape(parent_total, RANK, NRHS), precision=precise).reshape(leaf_total, RANK * NRHS) + leaf_far
    far_values = jnp.einsum("rlp,lrk->klp", basis_blocks, leaf_field.reshape(leaf_total, RANK, NRHS), precision=precise).reshape(NRHS, -1)
    device_points = sorted_points.reshape(3, N_LEAF, LEAVES_DEV, LEAF).transpose(1, 2, 0, 3)
    device_values = ordered.reshape(NRHS, N_LEAF, LEAVES_DEV, LEAF).transpose(1, 0, 2, 3)
    device_pairs = near_pairs.reshape(2, N_LEAF, NEAR_CAP).transpose(1, 0, 2)
    block_size = NEAR_CAP // 4
    near_parts = lax.map(lambda item: near_field(item[0], item[1], item[2], item[3], 4, block_size), (device_points, device_values, device_pairs, near_count))
    near_values = near_parts.transpose(2, 0, 1, 3).reshape(NRHS, -1)
    sorted_product = far_values + near_values
    return jnp.zeros_like(sorted_product).at[:, perm].set(sorted_product)
```

```python
import functools
import math

import jax
import jax.numpy as jnp
from jax import lax
from jax.experimental import pallas as pl
from jax.experimental.pallas import tpu as pltpu
from jax.sharding import PartitionSpec as P

LEAF = 64
RANK = 32
NRHS = 16
LANES = 128
ROWS = 48
SCALE = math.sqrt(math.log2(math.e))
F32 = jnp.float32
BF16 = jnp.bfloat16


def split2(x):
    hi = x.astype(BF16)
    return hi, (x - hi.astype(F32)).astype(BF16)


def dot(a, b):
    return jnp.dot(a, b, preferred_element_type=F32)


def dot_nt(a, b):
    return lax.dot_general(a, b, (((1,), (1,)), ((), ())), preferred_element_type=F32)


def dot3(a, b, product=dot):
    ah, al = split2(a)
    bh, bl = split2(b)
    return product(ah, bh) + product(al, bh) + product(ah, bl)


def lane_of(shape):
    return lax.broadcasted_iota(jnp.int32, shape, len(shape) - 1)


def pieces3(x):
    one = x.astype(BF16).astype(F32)
    rest = x - one
    two = rest.astype(BF16).astype(F32)
    return one, two, rest - two


def features(coords):
    width = coords.shape[1]
    row = lax.broadcasted_iota(jnp.int32, (8, width), 0)
    a = jnp.where(row < 3, (coords - 1.5) * SCALE, 0.0)
    norm = -0.5 * jnp.sum(a * a, axis=0, keepdims=True)
    a1, a2, a3 = pieces3(a)
    n1, n2, n3 = pieces3(norm)
    a4 = pltpu.roll(a2, 3, 0)
    up1 = pltpu.roll(a1, 3, 0)
    up3 = pltpu.roll(a3, 3, 0)
    one = jnp.ones((8, width), F32)
    zero = jnp.zeros((8, width), F32)

    def block(low, high, six, seven):
        return jnp.where(row < 3, low, jnp.where(row < 6, high, jnp.where(row == 6, six, seven)))

    target = (
        block(a1, up1, n1, n2),
        block(a2, a4, n3, one),
        block(a1, up3, one, one),
    )
    source = (
        block(a1, a4, one, one),
        block(a1, a4, one, n1),
        block(a3, up1, n2, n3),
    )
    return (
        jnp.concatenate(target + (zero,), axis=0),
        jnp.concatenate(source + (zero,), axis=0),
    )


def one_hot(low, width):
    return jnp.where(
        lax.broadcasted_iota(jnp.int32, (LANES, width), 0) == low, 1.0, 0.0
    ).astype(BF16)


def replicate_group(tile, group, which):
    kept = jnp.where(group == which, tile, 0.0)
    kept = kept + pltpu.roll(kept, 64, 1)
    return kept + pltpu.roll(kept, 32, 1)


def upward_kernel(
    peers,
    lists,
    rhs,
    points,
    order,
    basis,
    child,
    root,
    leaf_skel,
    parent_skel,
    root_skel,
    top,
    values,
    sorted_points,
    leaf_mom,
    parent_mom,
    leaf_coords,
    parent_coords,
    message,
    pad_points,
    table_values,
    table_points,
):
    count = rhs.shape[1]
    tiles = count // LANES
    parents = parent_mom.shape[0]
    pad_points[...] = jnp.zeros_like(pad_points)
    pad_points[0:3, :] = points[...]
    for h in range(tiles // 2):
        for wide, rows, source, table in ((16, 32, rhs, table_values), (8, 16, pad_points, table_points)):
            both = jnp.concatenate(
                [
                    source[:, 2 * h * LANES : (2 * h + 1) * LANES],
                    source[:, (2 * h + 1) * LANES : (2 * h + 2) * LANES],
                ],
                axis=0,
            )
            for at, piece in enumerate(pieces3(both)):
                table[h * rows : (h + 1) * rows, at * LANES : (at + 1) * LANES] = piece.astype(BF16)

    step = 256

    def gather(t, carry):
        at = pl.ds(pl.multiple_of(t * step, step), step)
        where_from = order[:, at]
        low = where_from & (LANES - 1)
        high = where_from >> 7
        hot = one_hot(low, step)
        hot3 = jnp.concatenate([hot, hot, hot], axis=0)
        got = dot(table_values[...], hot3)
        got_points = dot(table_points[...], hot3)
        total = jnp.zeros((16, step), F32)
        total_points = jnp.zeros((8, step), F32)
        for h in range(tiles):
            hit = high == h
            total = total + jnp.where(hit, got[h * 16 : (h + 1) * 16], 0.0)
            total_points = total_points + jnp.where(hit, got_points[h * 8 : (h + 1) * 8], 0.0)
        values[:, at] = total
        sorted_points[:, at] = total_points
        return carry

    lax.fori_loop(0, count // step, gather, 0)

    lane16 = lane_of((16, LANES))
    group16 = lane16 // RANK
    group8 = lane_of((8, LANES)) // RANK

    def leaves(g, carry):
        at = pl.ds(pl.multiple_of(g * LANES, LANES), LANES)
        vt = values[:, at]
        bt = basis[:, at]
        left = jnp.concatenate(
            [jnp.where(lane16 < LEAF, vt, 0.0), jnp.where(lane16 >= LEAF, vt, 0.0)], axis=0
        )
        both = dot3(left, jnp.concatenate([bt] * 4, axis=0), dot_nt)
        leaf_mom[2 * g] = both[:16]
        leaf_mom[2 * g + 1] = both[16:]
        pair = jnp.where(lane16 < RANK, both[:16], both[16:])
        parent_mom[g] = dot3(pair[:, : 2 * RANK], child[g])
        return carry

    lax.fori_loop(0, parents, leaves, 0, unroll=4)

    root4 = jnp.zeros((16, LANES), F32)
    for g in range(parents // 4):
        left = jnp.zeros((16, LANES), F32)
        for q in range(4):
            left = jnp.where(group16 == q, parent_mom[4 * g + q], left)
        root4 = root4 + dot3(left, root[g * LANES : (g + 1) * LANES])

    pad_points[...] = jnp.zeros_like(pad_points)
    pad_points[0:3, 0 : leaf_skel.shape[1]] = leaf_skel[...]
    for g in range(leaf_skel.shape[1] // LANES):
        tile = pad_points[:, g * LANES : (g + 1) * LANES]
        for q in range(4):
            leaf_coords[4 * g + q] = replicate_group(tile, group8, q)
    pad_points[0:3, 0 : parent_skel.shape[1]] = parent_skel[...]
    for g in range(parent_skel.shape[1] // LANES):
        tile = pad_points[:, g * LANES : (g + 1) * LANES]
        for q in range(4):
            parent_coords[4 * g + q] = replicate_group(tile, group8, q)

    pad_points[:, 0:LANES] = jnp.zeros((8, LANES), F32)
    pad_points[0:3, 0:RANK] = root_skel[...]
    pad_points[3:5, 0 : top.shape[1]] = top[...].astype(F32)
    root_data = pad_points[:, 0:LANES]

    def pack(d, carry):
        moments = jnp.zeros((16, LANES), F32)
        coords = jnp.zeros((8, LANES), F32)
        for q in range(4):
            level, slot = q // 2, q % 2
            node = lists[level * 2 * peers + 2 * d + slot]
            live = node >= 0
            safe = jnp.maximum(node, 0)
            mom_ref, coord_ref = (leaf_mom, leaf_coords) if level == 0 else (parent_mom, parent_coords)
            moments = jnp.where((group16 == q) & live, mom_ref[safe], moments)
            coords = jnp.where((group8 == q) & live, coord_ref[safe], coords)
        message[d, 0:16] = moments
        message[d, 16:24] = coords
        message[d, 24:40] = root4
        message[d, 40:48] = root_data
        return carry

    lax.fori_loop(0, peers, pack, 0, unroll=4)


def couple_kernel(
    used,
    near,
    leaf_pairs,
    parent_pairs,
    values,
    sorted_points,
    leaf_mom,
    parent_mom,
    leaf_coords,
    parent_coords,
    near_out,
    leaf_out,
    parent_out,
    near_left,
    near_right,
    near_values,
    leaf_left,
    leaf_right,
    leaf_pieces,
    parent_left,
    parent_right,
    parent_pieces,
):
    leaves = leaf_mom.shape[0]
    parents = parent_mom.shape[0]
    near_out[...] = jnp.zeros_like(near_out)
    leaf_out[...] = jnp.zeros_like(leaf_out)
    parent_out[...] = jnp.zeros_like(parent_out)
    lane16 = lane_of((16, LANES))
    group16 = lane16 // RANK
    lane32 = lane_of((32, LANES))
    group32 = lane32 // RANK
    lane64 = lane_of((64, LANES))

    def near_prep(g, carry):
        at = pl.ds(pl.multiple_of(g * LANES, LANES), LANES)
        target, source = features(sorted_points[:, at])
        turned = pltpu.roll(target, 64, 1)
        for j in range(2):
            low, high = (target, turned) if j == 0 else (turned, target)
            near_right[0, 2 * g + j] = jnp.where(lane32 < LEAF, low, 0.0).astype(BF16)
            near_right[1, 2 * g + j] = jnp.where(lane32 >= LEAF, high, 0.0).astype(BF16)
        across = jnp.concatenate([source] * 4, axis=0).T
        for j in range(2):
            part = across[64 * j : 64 * (j + 1)]
            near_left[0, 2 * g + j] = jnp.where(lane64 < RANK, part, 0.0).astype(BF16)[:, :64]
            near_left[1, 2 * g + j] = jnp.where(lane64 >= RANK, part, 0.0).astype(BF16)[:, :64]
        tile = values[:, at]
        spun = pltpu.roll(tile, 64, 1)
        for j in range(2):
            twice = jnp.where((lane16 < LEAF) == (j == 0), tile, spun)
            hi = twice.astype(BF16).astype(F32)
            both = jnp.where(lane16 < LEAF, hi, twice - hi).astype(BF16)
            near_values[2 * g + j] = jnp.concatenate([both, both], axis=1)
        return carry

    lax.fori_loop(0, leaves // 2, near_prep, 0, unroll=2)

    def far_prep(mom, coords, left, right, pieces, count):
        def body(n, carry):
            target, source = features(coords[n])
            across = jnp.concatenate([source] * 4, axis=0).T[:RANK]
            for q in range(4):
                right[q, n] = jnp.where(group32 == q, target, 0.0).astype(BF16)
                left[q, n] = jnp.where(group32 == q, across, 0.0).astype(BF16)
            m = mom[n]
            hi = m.astype(BF16).astype(F32)
            pieces[n] = jnp.where(group16 % 2 == 0, hi, m - hi).astype(BF16)
            return carry

        lax.fori_loop(0, count, body, 0, unroll=2)

    far_prep(leaf_mom, leaf_coords, leaf_left, leaf_right, leaf_pieces, leaves)
    far_prep(parent_mom, parent_coords, parent_left, parent_right, parent_pieces, parents)

    def far(pairs, left, right, pieces, out, unroll):
        total = pairs.shape[1]

        def body(c, carry):
            done = []
            for u in range(unroll):
                base = (c * unroll + u) * 4
                ts = [pairs[0, base + q] for q in range(4)]
                ss = [pairs[1, base + q] for q in range(4)]
                rhs = jnp.concatenate([right[q, ts[q]] for q in range(4)], axis=0)
                lhs = (left[0, ss[0]] + left[1, ss[1]]) + (left[2, ss[2]] + left[3, ss[3]])
                hi, lo = split2(jnp.exp2(dot(lhs, rhs)))
                weights = jnp.concatenate([hi, hi, lo, lo], axis=0)
                got = dot(jnp.concatenate([pieces[s] for s in ss], axis=0), weights)
                done.append((ts, got))
            for ts, got in done:
                for q in range(4):
                    part = got[16 * q : 16 * (q + 1)]
                    out[ts[q]] += jnp.where(group16 == q, part, 0.0)
            return carry

        lax.fori_loop(0, total // (4 * unroll), body, 0)

    far(leaf_pairs, leaf_left, leaf_right, leaf_pieces, leaf_out, 4)
    far(parent_pairs, parent_left, parent_right, parent_pieces, parent_out, 4)

    unroll = 8
    limit = used[0]

    def near_body(c, carry):
        done = []
        for u in range(unroll):
            base = (c * unroll + u) * 2
            t0, t1 = near[0, base], near[0, base + 1]
            s0, s1 = near[1, base], near[1, base + 1]
            rhs = jnp.concatenate([near_right[0, t0], near_right[1, t1]], axis=0)
            lhs = near_left[0, s0] + near_left[1, s1]
            hi, lo = split2(jnp.exp2(dot(lhs, rhs)))
            weights = jnp.concatenate([hi, hi, lo, lo], axis=0)
            got = dot(jnp.concatenate([near_values[s0], near_values[s1]], axis=0), weights)
            done.append((base, t0, t1, got))
        for base, t0, t1, got in done:
            near_out[t0] += jnp.where((lane16 < LEAF) & (base < limit), got[:16], 0.0)
            near_out[t1] += jnp.where((lane16 >= LEAF) & (base + 1 < limit), got[16:], 0.0)
        return carry

    chunk = 2 * unroll
    lax.fori_loop(0, (limit + chunk - 1) // chunk, near_body, 0)


def downward_kernel(
    peers,
    lists,
    arrived,
    order,
    basis,
    child,
    root,
    root_skel,
    near_in,
    leaf_in,
    parent_in,
    leaf_coords,
    parent_coords,
    product,
    leaf_acc,
    parent_acc,
    pad_root,
    sorted_product,
    scattered,
):
    count = product.shape[1]
    tiles = count // LANES
    parents = parent_acc.shape[0]
    me = lax.axis_index("leaf")
    leaf_acc[...] = leaf_in[...]
    parent_acc[...] = parent_in[...]
    pad_root[...] = jnp.zeros_like(pad_root)
    pad_root[0:3, 0:RANK] = root_skel[...]
    lane16 = lane_of((16, LANES))
    group16 = lane16 // RANK
    group8 = lane_of((8, LANES)) // RANK
    square = (LANES, LANES)
    diagonal = lax.broadcasted_iota(jnp.int32, square, 0) // RANK == lane_of(square) // RANK
    root_target = features(pad_root[...])[0].astype(BF16)
    top_targets = arrived[:, 43, :]
    top_sources = arrived[:, 44, :]
    used_lanes = lane_of(top_targets.shape) < TOP_WIDTH[0]
    mine = (top_targets == me.astype(F32)) & used_lanes

    def remote(d, field):
        moments = arrived[d, 0:16]
        source = features(arrived[d, 16:24])[1]
        across = jnp.concatenate([source] * 4, axis=0).T.astype(BF16)[:, :RANK]
        coords = jnp.zeros((8, LANES), F32)
        targets = []
        for q in range(4):
            level, slot = q // 2, q % 2
            node = jnp.maximum(lists[level * 2 * peers + 2 * d + slot], 0)
            targets.append(node)
            ref = leaf_coords if level == 0 else parent_coords
            coords = jnp.where(group8 == q, ref[node], coords)
        target = features(coords)[0].astype(BF16)
        matrix = jnp.where(diagonal, jnp.exp2(dot(across, target)), 0.0)
        got = dot3(moments, matrix)
        for q in range(4):
            acc = leaf_acc if q < 2 else parent_acc
            live = lists[(q // 2) * 2 * peers + 2 * d + q % 2] >= 0
            acc[targets[q]] += jnp.where((group16 == q) & live, got, 0.0)
        root_source = features(arrived[d, 40:48])[1]
        root_across = jnp.concatenate([root_source] * 4, axis=0).T.astype(BF16)[:RANK, :RANK]
        weight = jnp.sum(
            jnp.where(mine & (top_sources == d.astype(F32)), 1.0, 0.0), keepdims=True
        )
        root_matrix = jnp.exp2(dot(root_across, root_target))
        root_got = dot3(arrived[d, 24:40][:, :RANK], root_matrix)
        return field + weight * root_got

    field = lax.fori_loop(0, peers, remote, jnp.zeros((16, LANES), F32), unroll=4)
    field = jnp.where(group16 == 0, field, 0.0)

    for g in range(parents // 4):
        got = dot3(field, root[g * LANES : (g + 1) * LANES], dot_nt)
        for q in range(4):
            parent_acc[4 * g + q] += jnp.where(group16 == q, got, 0.0)

    def leaves(m, carry):
        at = pl.ds(pl.multiple_of(m * LANES, LANES), LANES)
        block = child[m]
        down = dot3(parent_acc[m], jnp.concatenate([block, block], axis=0), dot_nt)
        first = leaf_acc[2 * m] + jnp.where(group16 == 0, down, 0.0)
        second = leaf_acc[2 * m + 1] + jnp.where(group16 == 1, down, 0.0)
        bt = basis[:, at]
        both = dot3(
            jnp.concatenate([first, second], axis=0), jnp.concatenate([bt] * 4, axis=0)
        )
        x, y = near_in[2 * m], near_in[2 * m + 1]
        x = x + pltpu.roll(x, 64, 1) + both[:16]
        y = y + pltpu.roll(y, 64, 1) + both[16:]
        sorted_product[:, at] = jnp.where(lane16 < LEAF, x, y)
        return carry

    lax.fori_loop(0, parents, leaves, 0, unroll=4)

    step = 256
    scattered[...] = jnp.zeros_like(scattered)

    def scatter(t, carry):
        at = pl.ds(pl.multiple_of(t * step, step), step)
        where_to = order[:, at]
        hot = one_hot(where_to & (LANES - 1), step)
        high = where_to >> 7
        z = sorted_product[:, at]
        hi = z.astype(BF16).astype(F32)
        lo = z - hi
        for piece in (hi, lo):
            spread = jnp.concatenate(
                [jnp.where(high == h, piece, 0.0).astype(BF16) for h in range(tiles)], axis=0
            )
            scattered[...] += dot_nt(spread, hot)
        return carry

    lax.fori_loop(0, count // step, scatter, 0)
    for h in range(tiles):
        product[:, h * LANES : (h + 1) * LANES] = scattered[h * 16 : (h + 1) * 16]


TOP_WIDTH = [8]
VM = pl.BlockSpec(memory_space=pltpu.VMEM)
SM = pl.BlockSpec(memory_space=pltpu.SMEM)
PARAMS = pltpu.CompilerParams(vmem_limit_bytes=48 * 1024 * 1024)


def shape(*dims, dtype=F32):
    return jax.ShapeDtypeStruct(dims, dtype)


def shards(
    right_sides,
    point_coords,
    cluster_order,
    leaf_basis,
    child_transfer,
    root_transfer,
    leaf_skeleton,
    parent_skeleton,
    root_skeleton,
    near_pairs,
    near_count,
    leaf_send,
    leaf_receive,
    parent_send,
    parent_receive,
    leaf_pairs,
    parent_pairs,
    top_pairs,
):
    peers = lax.axis_size("leaf")
    count = right_sides.shape[1]
    leaves = count // LEAF
    parents = leaves // 2
    TOP_WIDTH[0] = top_pairs.shape[1]
    order = cluster_order.reshape(1, count)
    child = jnp.tile(child_transfer.reshape(parents, 2 * RANK, RANK), (1, 1, 4))
    root = jnp.tile(root_transfer.reshape(parents * RANK, RANK), (1, 4))
    sends = jnp.concatenate([leaf_send.reshape(-1), parent_send.reshape(-1)])
    receives = jnp.concatenate([leaf_receive.reshape(-1), parent_receive.reshape(-1)])
    values, points, leaf_mom, parent_mom, leaf_coords, parent_coords, message = pl.pallas_call(
        functools.partial(upward_kernel, peers),
        out_shape=(
            shape(16, count),
            shape(8, count),
            shape(leaves, 16, LANES),
            shape(parents, 16, LANES),
            shape(leaves, 8, LANES),
            shape(parents, 8, LANES),
            shape(peers, ROWS, LANES),
        ),
        in_specs=[SM] + [VM] * 10,
        out_specs=(VM,) * 7,
        scratch_shapes=[
            pltpu.VMEM((8, count), F32),
            pltpu.VMEM((16 * (count // LANES), 3 * LANES), BF16),
            pltpu.VMEM((8 * (count // LANES), 3 * LANES), BF16),
        ],
        compiler_params=PARAMS,
        name="upward",
    )(
        sends,
        right_sides,
        point_coords,
        order,
        leaf_basis,
        child,
        root,
        leaf_skeleton,
        parent_skeleton,
        root_skeleton,
        top_pairs,
    )
    arrived = lax.all_to_all(message, "leaf", split_axis=0, concat_axis=0, tiled=True)
    near_sum, leaf_sum, parent_sum = pl.pallas_call(
        couple_kernel,
        out_shape=(
            shape(leaves, 16, LANES),
            shape(leaves, 16, LANES),
            shape(parents, 16, LANES),
        ),
        in_specs=[SM] * 4 + [VM] * 6,
        out_specs=(VM,) * 3,
        scratch_shapes=[
            pltpu.VMEM((2, leaves, 64, 64), BF16),
            pltpu.VMEM((2, leaves, 32, LANES), BF16),
            pltpu.VMEM((leaves, 16, 256), BF16),
            pltpu.VMEM((4, leaves, 32, LANES), BF16),
            pltpu.VMEM((4, leaves, 32, LANES), BF16),
            pltpu.VMEM((leaves, 16, LANES), BF16),
            pltpu.VMEM((4, parents, 32, LANES), BF16),
            pltpu.VMEM((4, parents, 32, LANES), BF16),
            pltpu.VMEM((parents, 16, LANES), BF16),
        ],
        compiler_params=PARAMS,
        cost_estimate=pl.CostEstimate(
            flops=20_000_000_000, bytes_accessed=8_000_000, transcendentals=4_000_000
        ),
        name="couple",
    )(
        near_count,
        near_pairs,
        leaf_pairs,
        parent_pairs,
        values,
        points,
        leaf_mom,
        parent_mom,
        leaf_coords,
        parent_coords,
    )
    return pl.pallas_call(
        functools.partial(downward_kernel, peers),
        out_shape=shape(16, count),
        in_specs=[SM] + [VM] * 11,
        out_specs=VM,
        scratch_shapes=[
            pltpu.VMEM((leaves, 16, LANES), F32),
            pltpu.VMEM((parents, 16, LANES), F32),
            pltpu.VMEM((8, LANES), F32),
            pltpu.VMEM((16, count), F32),
            pltpu.VMEM((16 * (count // LANES), LANES), F32),
        ],
        compiler_params=PARAMS,
        name="downward",
    )(
        receives,
        arrived,
        order,
        leaf_basis,
        child,
        root,
        root_skeleton,
        near_sum,
        leaf_sum,
        parent_sum,
        leaf_coords,
        parent_coords,
    )


def solution(mesh):
    leaf = ("groups", "leaf")
    columns = P(None, leaf)
    nodes = P(leaf, None, None)
    in_specs = (
        columns,
        columns,
        P(leaf),
        columns,
        P(leaf, None),
        P(leaf, None),
        columns,
        columns,
        columns,
        columns,
        P(leaf),
        nodes,
        nodes,
        nodes,
        nodes,
        columns,
        columns,
        columns,
    )
    return jax.shard_map(
        shards, mesh=mesh, in_specs=in_specs, out_specs=columns, check_vma=False
    )
```

```python
import functools
import math

import jax
import jax.numpy as jnp
from jax import lax
from jax.experimental import pallas as pl
from jax.experimental.pallas import tpu as pltpu
from jax.sharding import PartitionSpec as P

LEAF = 64
RANK = 32
NRHS = 16
LANES = 128
ROWS = 48
SCALE = math.sqrt(math.log2(math.e))
F32 = jnp.float32
BF16 = jnp.bfloat16


def split2(x):
    hi = x.astype(BF16)
    return hi, (x - hi.astype(F32)).astype(BF16)


def dot(a, b):
    return jnp.dot(a, b, preferred_element_type=F32)


def dot_nt(a, b):
    return lax.dot_general(a, b, (((1,), (1,)), ((), ())), preferred_element_type=F32)


def dot3(a, b, product=dot):
    ah, al = split2(a)
    bh, bl = split2(b)
    return product(ah, bh) + (product(al, bh) + product(ah, bl))


def lane_of(shape):
    return lax.broadcasted_iota(jnp.int32, shape, len(shape) - 1)


def pieces3(x):
    one = x.astype(BF16).astype(F32)
    rest = x - one
    two = rest.astype(BF16).astype(F32)
    return one, two, rest - two


def features(coords):
    width = coords.shape[1]
    row = lax.broadcasted_iota(jnp.int32, (8, width), 0)
    a = jnp.where(row < 3, coords * SCALE, 0.0)
    norm = -0.5 * jnp.sum(a * a, axis=0, keepdims=True)
    a1, a2, a3 = pieces3(a)
    n1, n2, n3 = pieces3(norm)
    a4 = pltpu.roll(a2, 3, 0)
    up1 = pltpu.roll(a1, 3, 0)
    up3 = pltpu.roll(a3, 3, 0)
    one = jnp.ones((8, width), F32)
    zero = jnp.zeros((8, width), F32)

    def block(low, high, six, seven):
        return jnp.where(row < 3, low, jnp.where(row < 6, high, jnp.where(row == 6, six, seven)))

    target = (
        block(a1, up1, n1, n2),
        block(a2, a4, n3, one),
        block(a1, up3, one, one),
    )
    source = (
        block(a1, a4, one, one),
        block(a1, a4, one, n1),
        block(a3, up1, n2, n3),
    )
    return (
        jnp.concatenate(target + (zero,), axis=0),
        jnp.concatenate(source + (zero,), axis=0),
    )


def one_hot(low, width):
    return jnp.where(
        lax.broadcasted_iota(jnp.int32, (LANES, width), 0) == low, 1.0, 0.0
    ).astype(BF16)


def wide(block):
    return jnp.concatenate([block] * 4, axis=1)


def replicate_group(tile, group, which):
    kept = jnp.where(group == which, tile, 0.0)
    kept = kept + pltpu.roll(kept, 64, 1)
    return kept + pltpu.roll(kept, 32, 1)


def upward_kernel(
    peers,
    leaf_send,
    parent_send,
    rhs,
    points,
    order,
    basis,
    child,
    root,
    leaf_skel,
    parent_skel,
    root_skel,
    top,
    values,
    nodes,
    message,
    pad_points,
    table,
):
    count = rhs.shape[1]
    tiles = count // LANES
    parents = child.shape[0]
    leaves = 2 * parents
    pad_points[...] = jnp.zeros_like(pad_points)
    pad_points[0:3, :] = points[...] - 1.5
    for h in range(tiles // 2):
        for source, rows, at in ((rhs, 32, 0), (pad_points, 16, 16 * tiles)):
            both = jnp.concatenate(
                [
                    source[:, 2 * h * LANES : (2 * h + 1) * LANES],
                    source[:, (2 * h + 1) * LANES : (2 * h + 2) * LANES],
                ],
                axis=0,
            )
            hi, lo = split2(both)
            span = slice(at + h * rows, at + (h + 1) * rows)
            table[span, 0:LANES] = hi
            table[span, LANES : 2 * LANES] = lo

    step = 256

    def gather(t, carry):
        at = pl.ds(pl.multiple_of(t * step, step), step)
        where_from = order[:, at]
        high = where_from >> 7
        hot = one_hot(where_from & (LANES - 1), step)
        got = dot(table[...], jnp.concatenate([hot, hot], axis=0))
        total = jnp.zeros((16, step), F32)
        total_points = jnp.zeros((8, step), F32)
        for h in range(tiles):
            hit = high == h
            total = jnp.where(hit, got[h * 16 : (h + 1) * 16], total)
            first = 16 * tiles + h * 8
            total_points = jnp.where(hit, got[first : first + 8], total_points)
        values[0:16, at] = total
        values[16:24, at] = total_points
        return carry

    lax.fori_loop(0, count // step, gather, 0)

    lane16 = lane_of((16, LANES))
    group16 = lane16 // RANK
    group8 = lane_of((8, LANES)) // RANK
    batch = 8

    def moments(c, carry):
        found = []
        for u in range(batch):
            g = c * batch + u
            at = pl.ds(pl.multiple_of(g * LANES, LANES), LANES)
            vt = values[0:16, at]
            left = jnp.concatenate(
                [jnp.where(lane16 < LEAF, vt, 0.0), jnp.where(lane16 >= LEAF, vt, 0.0)], axis=0
            )
            found.append(dot3(left, jnp.concatenate([basis[:, at]] * 4, axis=0), dot_nt))
        for u, both in enumerate(found):
            g = c * batch + u
            nodes[2 * g, 0:16] = both[:16]
            nodes[2 * g + 1, 0:16] = both[16:]
        raised = []
        for u, both in enumerate(found):
            pair = jnp.where(lane16 < RANK, both[:16], both[16:])
            raised.append(dot3(pair[:, : 2 * RANK], wide(child[c * batch + u])))
        for u, up in enumerate(raised):
            nodes[leaves + c * batch + u, 0:16] = up
        return carry

    lax.fori_loop(0, parents // batch, moments, 0)

    root4 = jnp.zeros((16, LANES), F32)
    for g in range(parents // 4):
        left = jnp.zeros((16, LANES), F32)
        for q in range(4):
            left = jnp.where(group16 == q, nodes[leaves + 4 * g + q, 0:16], left)
        root4 = root4 + dot3(left, wide(root[g * LANES : (g + 1) * LANES]))

    for skeleton, first in ((leaf_skel, 0), (parent_skel, leaves)):
        pad_points[0:3, 0 : skeleton.shape[1]] = skeleton[...] - 1.5
        for g in range(skeleton.shape[1] // LANES):
            tile = pad_points[:, g * LANES : (g + 1) * LANES]
            for q in range(4):
                nodes[first + 4 * g + q, 16:24] = replicate_group(tile, group8, q)

    pad_points[:, 0:LANES] = jnp.zeros((8, LANES), F32)
    pad_points[0:3, 0:RANK] = root_skel[...] - 1.5
    pad_points[3:5, 0 : top.shape[1]] = top[...].astype(F32)
    root_data = replicate_group(pad_points[:, 0:LANES], group8, 0)

    group24 = lane_of((24, LANES)) // RANK

    def pack(d, carry):
        block = jnp.zeros((24, LANES), F32)
        for q in range(4):
            send = leaf_send if q < 2 else parent_send
            node = send[q % 2, d]
            safe = jnp.maximum(node, 0) + (0 if q < 2 else leaves)
            block = jnp.where((group24 == q) & (node >= 0), nodes[safe], block)
        message[d, 0:24] = block
        message[d, 24:40] = root4
        message[d, 40:48] = root_data
        return carry

    lax.fori_loop(0, peers, pack, 0, unroll=4)


def couple_kernel(
    peers,
    top_width,
    used,
    near,
    leaf_pairs,
    parent_pairs,
    leaf_receive,
    parent_receive,
    arrived,
    values,
    nodes,
    order,
    basis,
    child,
    root,
    root_skel,
    product,
    near_sum,
    far_sum,
    near_left,
    near_right,
    near_values,
    far_left,
    far_right,
    far_pieces,
    pad_root,
    sorted_product,
    scattered,
):
    count = product.shape[1]
    tiles = count // LANES
    parents = child.shape[0]
    leaves = 2 * parents
    near_sum[...] = jnp.zeros_like(near_sum)
    far_sum[...] = jnp.zeros_like(far_sum)
    lane16 = lane_of((16, LANES))
    group16 = lane16 // RANK
    group8 = lane_of((8, LANES)) // RANK
    lane32 = lane_of((32, LANES))
    group32 = lane32 // RANK
    lane64 = lane_of((64, LANES))

    def near_prep(g, carry):
        at = pl.ds(pl.multiple_of(g * LANES, LANES), LANES)
        target, source = features(values[16:24, at])
        turned = pltpu.roll(target, 64, 1)
        across = jnp.concatenate([source] * 4, axis=0).T
        tile = values[0:16, at]
        spun = pltpu.roll(tile, 64, 1)
        for j in range(2):
            low, high = (target, turned) if j == 0 else (turned, target)
            near_right[0, 2 * g + j] = jnp.where(lane32 < LEAF, low, 0.0).astype(BF16)
            near_right[1, 2 * g + j] = jnp.where(lane32 >= LEAF, high, 0.0).astype(BF16)
            part = across[64 * j : 64 * (j + 1)]
            near_left[0, 2 * g + j] = jnp.where(lane64 < RANK, part, 0.0).astype(BF16)[:, :64]
            near_left[1, 2 * g + j] = jnp.where(lane64 >= RANK, part, 0.0).astype(BF16)[:, :64]
            twice = jnp.where((lane16 < LEAF) == (j == 0), tile, spun)
            hi = twice.astype(BF16).astype(F32)
            both = jnp.where(lane16 < LEAF, hi, twice - hi).astype(BF16)
            near_values[2 * g + j] = jnp.concatenate([both, both], axis=1)
        return carry

    lax.fori_loop(0, parents, near_prep, 0, unroll=4)

    def far_prep(g, carry):
        tile = jnp.zeros((8, LANES), F32)
        for q in range(4):
            tile = jnp.where(group8 == q, nodes[4 * g + q, 16:24], tile)
        across = jnp.concatenate([features(tile)[1]] * 4, axis=0).T
        for j in range(4):
            n = 4 * g + j
            target = features(nodes[n, 16:24])[0]
            part = across[32 * j : 32 * (j + 1)]
            for q in range(4):
                far_right[q, n] = jnp.where(group32 == q, target, 0.0).astype(BF16)
                far_left[q, n] = jnp.where(group32 == q, part, 0.0).astype(BF16)
            m = nodes[n, 0:16]
            hi = m.astype(BF16).astype(F32)
            far_pieces[n] = jnp.where(group16 % 2 == 0, hi, m - hi).astype(BF16)
        return carry

    lax.fori_loop(0, (leaves + parents) // 4, far_prep, 0, unroll=2)

    def far(pairs, first):
        groups = pairs.shape[1] // 4
        unroll = 16 if groups % 16 == 0 else 1

        def body(c, carry):
            ids, fields = [], []
            for u in range(unroll):
                base = (c * unroll + u) * 4
                ts = [pairs[0, base + q] + first for q in range(4)]
                ss = [pairs[1, base + q] + first for q in range(4)]
                rhs = jnp.concatenate([far_right[q, ts[q]] for q in range(4)], axis=0)
                lhs = (far_left[0, ss[0]] + far_left[1, ss[1]]) + (
                    far_left[2, ss[2]] + far_left[3, ss[3]]
                )
                ids.append((ts, ss))
                fields.append(dot(lhs, rhs))
            fields = [split2(jnp.exp2(e)) for e in fields]
            gots = [
                dot(
                    jnp.concatenate([far_pieces[s] for s in ss], axis=0),
                    jnp.concatenate([hi, hi, lo, lo], axis=0),
                )
                for (ts, ss), (hi, lo) in zip(ids, fields)
            ]
            for (ts, ss), got in zip(ids, gots):
                for q in range(4):
                    part = got[16 * q : 16 * (q + 1)]
                    far_sum[ts[q]] += jnp.where(group16 == q, part, 0.0)
            return carry

        lax.fori_loop(0, groups // unroll, body, 0)

    far(leaf_pairs, 0)
    far(parent_pairs, leaves)

    near_width = near.shape[1]
    unroll = 24 if near_width % 48 == 0 else 1
    limit = used[0]

    def near_body(c, carry):
        fields, gots = [], []
        for u in range(unroll):
            base = (c * unroll + u) * 2
            rhs = jnp.concatenate(
                [near_right[0, near[0, base]], near_right[1, near[0, base + 1]]], axis=0
            )
            fields.append(dot(near_left[0, near[1, base]] + near_left[1, near[1, base + 1]], rhs))
        fields = [split2(jnp.exp2(e)) for e in fields]
        for u, (hi, lo) in enumerate(fields):
            base = (c * unroll + u) * 2
            lhs = jnp.concatenate(
                [near_values[near[1, base]], near_values[near[1, base + 1]]], axis=0
            )
            gots.append(dot(lhs, jnp.concatenate([hi, hi, lo, lo], axis=0)))
        for u, got in enumerate(gots):
            base = (c * unroll + u) * 2
            near_sum[near[0, base]] += jnp.where(
                (lane16 < LEAF) & (base < limit), got[:16], 0.0
            )
            near_sum[near[0, base + 1]] += jnp.where(
                (lane16 >= LEAF) & (base + 1 < limit), got[16:], 0.0
            )
        return carry

    chunk = 2 * unroll
    lax.fori_loop(0, (limit + chunk - 1) // chunk, near_body, 0)

    me = lax.axis_index("leaf")
    pad_root[...] = jnp.zeros_like(pad_root)
    pad_root[0:3, 0:RANK] = root_skel[...] - 1.5
    square = (LANES, LANES)
    diagonal = lax.broadcasted_iota(jnp.int32, square, 0) // RANK == lane_of(square) // RANK
    root_target = features(pad_root[...])[0].astype(BF16)
    top_targets = arrived[:, 43, :]
    top_sources = arrived[:, 44, :]
    mine = (top_targets == me.astype(F32)) & (lane_of(top_targets.shape) < top_width)
    batch = 8 if peers % 8 == 0 else 4

    def turn(source):
        return jnp.concatenate([source] * 4, axis=0).T.astype(BF16)[:, :RANK]

    def remote(c, field):
        all_targets, powers = [], []
        for u in range(batch):
            d = c * batch + u
            across = turn(features(arrived[d, 16:24])[1])
            coords = jnp.zeros((8, LANES), F32)
            targets = []
            for q in range(4):
                receive = leaf_receive if q < 2 else parent_receive
                node = receive[q % 2, d]
                safe = jnp.maximum(node, 0) + (0 if q < 2 else leaves)
                targets.append((safe, node >= 0))
                coords = jnp.where(group8 == q, nodes[safe, 16:24], coords)
            all_targets.append(targets)
            powers.append(dot(across, features(coords)[0].astype(BF16)))
        root_powers, root_moments = [], []
        for v in range(batch // 4):
            coords = jnp.zeros((8, LANES), F32)
            moments = jnp.zeros((16, LANES), F32)
            for q in range(4):
                d = c * batch + 4 * v + q
                weight = jnp.sum(
                    jnp.where(mine & (top_sources == d.astype(F32)), 1.0, 0.0), keepdims=True
                )
                coords = jnp.where(group8 == q, arrived[d, 40:48], coords)
                moments = jnp.where(group16 == q, arrived[d, 24:40] * weight, moments)
            root_powers.append(dot(turn(features(coords)[1]), root_target))
            root_moments.append(moments)
        gots = [
            dot3(arrived[c * batch + u, 0:16], jnp.where(diagonal, jnp.exp2(e), 0.0))
            for u, e in enumerate(powers)
        ]
        for moments, e in zip(root_moments, root_powers):
            field = field + dot3(moments, jnp.exp2(e))
        for targets, got in zip(all_targets, gots):
            for q, (safe, live) in enumerate(targets):
                far_sum[safe] += jnp.where((group16 == q) & live, got, 0.0)
        return field

    field = lax.fori_loop(0, peers // batch, remote, jnp.zeros((16, LANES), F32))
    field = jnp.where(group16 == 0, field, 0.0)

    for g in range(parents // 4):
        got = dot3(field, wide(root[g * LANES : (g + 1) * LANES]), dot_nt)
        for q in range(4):
            far_sum[leaves + 4 * g + q] += jnp.where(group16 == q, got, 0.0)

    lower = 8

    def finish(c, carry):
        downs, boths = [], []
        for u in range(lower):
            m = c * lower + u
            block = wide(child[m])
            downs.append(
                dot3(far_sum[leaves + m], jnp.concatenate([block, block], axis=0), dot_nt)
            )
        for u, down in enumerate(downs):
            m = c * lower + u
            at = pl.ds(pl.multiple_of(m * LANES, LANES), LANES)
            first = far_sum[2 * m] + jnp.where(group16 == 0, down, 0.0)
            second = far_sum[2 * m + 1] + jnp.where(group16 == 1, down, 0.0)
            boths.append(
                dot3(
                    jnp.concatenate([first, second], axis=0),
                    jnp.concatenate([basis[:, at]] * 4, axis=0),
                )
            )
        for u, both in enumerate(boths):
            m = c * lower + u
            at = pl.ds(pl.multiple_of(m * LANES, LANES), LANES)
            x, y = near_sum[2 * m], near_sum[2 * m + 1]
            x = x + pltpu.roll(x, 64, 1) + both[:16]
            y = y + pltpu.roll(y, 64, 1) + both[16:]
            sorted_product[:, at] = jnp.where(lane16 < LEAF, x, y)
        return carry

    lax.fori_loop(0, parents // lower, finish, 0)

    step = 512
    scattered[...] = jnp.zeros_like(scattered)

    def scatter(t, carry):
        at = pl.ds(pl.multiple_of(t * step, step), step)
        where_to = order[:, at]
        hot = one_hot(where_to & (LANES - 1), step)
        high = where_to >> 7
        z = sorted_product[:, at]
        hi = z.astype(BF16).astype(F32)
        both = jnp.concatenate([hi, z - hi], axis=1)
        high2 = jnp.concatenate([high, high], axis=1)
        spread = jnp.concatenate(
            [jnp.where(high2 == h, both, 0.0).astype(BF16) for h in range(tiles)], axis=0
        )
        scattered[...] += dot_nt(spread, jnp.concatenate([hot, hot], axis=1))
        return carry

    lax.fori_loop(0, count // step, scatter, 0)
    for h in range(tiles):
        product[:, h * LANES : (h + 1) * LANES] = scattered[h * 16 : (h + 1) * 16]


VM = pl.BlockSpec(memory_space=pltpu.VMEM)
SM = pl.BlockSpec(memory_space=pltpu.SMEM)
PARAMS = pltpu.CompilerParams(vmem_limit_bytes=28 * 1024 * 1024)


def shape(*dims, dtype=F32):
    return jax.ShapeDtypeStruct(dims, dtype)


def shards(
    right_sides,
    point_coords,
    cluster_order,
    leaf_basis,
    child_transfer,
    root_transfer,
    leaf_skeleton,
    parent_skeleton,
    root_skeleton,
    near_pairs,
    near_count,
    leaf_send,
    leaf_receive,
    parent_send,
    parent_receive,
    leaf_pairs,
    parent_pairs,
    top_pairs,
):
    peers = lax.axis_size("leaf")
    count = right_sides.shape[1]
    leaves = count // LEAF
    parents = leaves // 2
    both = leaves + parents
    order = cluster_order.reshape(1, count)
    child = child_transfer.reshape(parents, 2 * RANK, RANK)
    root = root_transfer.reshape(parents * RANK, RANK)

    def slots(plan):
        return plan.transpose(0, 2, 1).reshape(2, peers)

    values, nodes, message = pl.pallas_call(
        functools.partial(upward_kernel, peers),
        out_shape=(
            shape(24, count),
            shape(both, 24, LANES),
            shape(peers, ROWS, LANES),
        ),
        in_specs=[SM] * 2 + [VM] * 10,
        out_specs=(VM,) * 3,
        scratch_shapes=[
            pltpu.VMEM((8, count), F32),
            pltpu.VMEM((24 * (count // LANES), 2 * LANES), BF16),
        ],
        compiler_params=PARAMS,
        name="upward",
    )(
        slots(leaf_send),
        slots(parent_send),
        right_sides,
        point_coords,
        order,
        leaf_basis,
        child,
        root,
        leaf_skeleton,
        parent_skeleton,
        root_skeleton,
        top_pairs,
    )
    arrived = lax.all_to_all(message, "leaf", split_axis=0, concat_axis=0, tiled=True)
    return pl.pallas_call(
        functools.partial(couple_kernel, peers, top_pairs.shape[1]),
        out_shape=shape(16, count),
        in_specs=[SM] * 6 + [VM] * 8,
        out_specs=VM,
        scratch_shapes=[
            pltpu.VMEM((leaves, 16, LANES), F32),
            pltpu.VMEM((both, 16, LANES), F32),
            pltpu.VMEM((2, leaves, 64, 64), BF16),
            pltpu.VMEM((2, leaves, 32, LANES), BF16),
            pltpu.VMEM((leaves, 16, 256), BF16),
            pltpu.VMEM((4, both, 32, LANES), BF16),
            pltpu.VMEM((4, both, 32, LANES), BF16),
            pltpu.VMEM((both, 16, LANES), BF16),
            pltpu.VMEM((8, LANES), F32),
            pltpu.VMEM((16, count), F32),
            pltpu.VMEM((16 * (count // LANES), LANES), F32),
        ],
        compiler_params=PARAMS,
        name="couple",
    )(
        near_count,
        near_pairs,
        leaf_pairs,
        parent_pairs,
        slots(leaf_receive),
        slots(parent_receive),
        arrived,
        values,
        nodes,
        order,
        leaf_basis,
        child,
        root,
        root_skeleton,
    )


def solution(mesh):
    leaf = ("groups", "leaf")
    columns = P(None, leaf)
    nodes = P(leaf, None, None)
    in_specs = (
        columns,
        columns,
        P(leaf),
        columns,
        P(leaf, None),
        P(leaf, None),
        columns,
        columns,
        columns,
        columns,
        P(leaf),
        nodes,
        nodes,
        nodes,
        nodes,
        columns,
        columns,
        columns,
    )
    return jax.shard_map(
        shards, mesh=mesh, in_specs=in_specs, out_specs=columns, check_vma=False
    )
```

```python
import functools
import math

import jax
import jax.numpy as jnp
from jax import lax
from jax.experimental import pallas as pl
from jax.experimental.pallas import tpu as pltpu
from jax.sharding import PartitionSpec as P

LEAF = 64
RANK = 32
NRHS = 16
LANES = 128
ROWS = 24
SCALE = math.sqrt(math.log2(math.e))
F32 = jnp.float32
BF16 = jnp.bfloat16


def split2(x):
    hi = x.astype(BF16)
    return hi, (x - hi.astype(F32)).astype(BF16)


def dot(a, b):
    return jnp.dot(a, b, preferred_element_type=F32)


def dot_nt(a, b):
    return lax.dot_general(a, b, (((1,), (1,)), ((), ())), preferred_element_type=F32)


def dot3(a, b, product=dot):
    ah, al = split2(a)
    bh, bl = split2(b)
    return product(ah, bh) + (product(al, bh) + product(ah, bl))


def lane_of(shape):
    return lax.broadcasted_iota(jnp.int32, shape, len(shape) - 1)


def pieces3(x):
    one = x.astype(BF16).astype(F32)
    rest = x - one
    two = rest.astype(BF16).astype(F32)
    return one, two, rest - two


def features(coords):
    width = coords.shape[1]
    row = lax.broadcasted_iota(jnp.int32, (8, width), 0)
    a = jnp.where(row < 3, coords * SCALE, 0.0)
    norm = -0.5 * jnp.sum(a * a, axis=0, keepdims=True)
    a1, a2, a3 = pieces3(a)
    n1, n2, n3 = pieces3(norm)
    a4 = pltpu.roll(a2, 3, 0)
    up1 = pltpu.roll(a1, 3, 0)
    up3 = pltpu.roll(a3, 3, 0)
    one = jnp.ones((8, width), F32)
    zero = jnp.zeros((8, width), F32)

    def block(low, high, six, seven):
        return jnp.where(row < 3, low, jnp.where(row < 6, high, jnp.where(row == 6, six, seven)))

    target = (
        block(a1, up1, n1, n2),
        block(a2, a4, n3, one),
        block(a1, up3, one, one),
    )
    source = (
        block(a1, a4, one, one),
        block(a1, a4, one, n1),
        block(a3, up1, n2, n3),
    )
    return (
        jnp.concatenate(target + (zero,), axis=0),
        jnp.concatenate(source + (zero,), axis=0),
    )


def one_hot(low, width):
    return jnp.where(
        lax.broadcasted_iota(jnp.int32, (LANES, width), 0) == low, 1.0, 0.0
    ).astype(BF16)


def wide(block):
    return jnp.concatenate([block] * 4, axis=1)


def replicate_group(tile, group, which):
    kept = jnp.where(group == which, tile, 0.0)
    kept = kept + pltpu.roll(kept, 64, 1)
    return kept + pltpu.roll(kept, 32, 1)


def pick(chosen, x):
    return sum(dot(chosen, piece.astype(BF16)) for piece in pieces3(x))


def fold_maps():
    down = lax.broadcasted_iota(jnp.int32, (8, 16), 1) // 4 + 4
    down = down == lax.broadcasted_iota(jnp.int32, (8, 16), 0)
    back = lax.broadcasted_iota(jnp.int32, (16, 8), 0) // 4 + 4
    back = back == lax.broadcasted_iota(jnp.int32, (16, 8), 1)
    return (
        jnp.where(down, 1.0, 0.0).astype(BF16),
        jnp.where(back, 1.0, 0.0).astype(BF16),
    )


def upward_kernel(
    peers,
    leaf_send,
    parent_send,
    rhs,
    points,
    order,
    basis,
    child,
    root,
    leaf_skel,
    parent_skel,
    root_skel,
    top,
    values,
    nodes,
    arrived,
    pad_points,
    table,
    point_table,
    message,
    send_sems,
    receive_sems,
):
    me = lax.axis_index("leaf")
    barrier = pltpu.get_barrier_semaphore()

    def greet(k, carry):
        pl.semaphore_signal(
            barrier,
            inc=1,
            device_id={"leaf": lax.rem(me + k, peers)},
            device_id_type=pl.DeviceIdType.MESH,
        )
        return carry

    lax.fori_loop(1, peers, greet, 0)
    count = rhs.shape[1]
    tiles = count // LANES
    parents = child.shape[0]
    leaves = 2 * parents
    pad_points[...] = jnp.zeros_like(pad_points)
    pad_points[0:3, :] = points[...] - 1.5
    for h in range(tiles // 2):
        for source, rows, into in ((rhs, 32, table), (pad_points, 16, point_table)):
            both = jnp.concatenate(
                [
                    source[:, 2 * h * LANES : (2 * h + 1) * LANES],
                    source[:, (2 * h + 1) * LANES : (2 * h + 2) * LANES],
                ],
                axis=0,
            )
            hi, lo = split2(both)
            span = slice(h * rows, (h + 1) * rows)
            into[span, 0:LANES] = hi
            into[span, LANES : 2 * LANES] = lo

    step = 256

    def gather(source, first, rows):
        def body(t, carry):
            at = pl.ds(pl.multiple_of(t * step, step), step)
            where_from = order[:, at]
            high = where_from >> 7
            hot = one_hot(where_from & (LANES - 1), step)
            got = dot(source[...], jnp.concatenate([hot, hot], axis=0))
            total = jnp.zeros((rows, step), F32)
            for h in range(tiles):
                total = jnp.where(high == h, got[h * rows : (h + 1) * rows], total)
            values[first : first + rows, at] = total
            return carry

        lax.fori_loop(0, count // step, body, 0)

    gather(table, 0, 16)

    lane16 = lane_of((16, LANES))
    group16 = lane16 // RANK
    group8 = lane_of((8, LANES)) // RANK
    batch = 8

    def moments(c, carry):
        found = []
        for u in range(batch):
            g = c * batch + u
            at = pl.ds(pl.multiple_of(g * LANES, LANES), LANES)
            vt = values[0:16, at]
            left = jnp.concatenate(
                [jnp.where(lane16 < LEAF, vt, 0.0), jnp.where(lane16 >= LEAF, vt, 0.0)], axis=0
            )
            found.append(dot3(left, jnp.concatenate([basis[:, at]] * 4, axis=0), dot_nt))
        for u, both in enumerate(found):
            g = c * batch + u
            nodes[2 * g, 0:16] = both[:16]
            nodes[2 * g + 1, 0:16] = both[16:]
        raised = []
        for u, both in enumerate(found):
            pair = jnp.where(lane16 < RANK, both[:16], both[16:])
            raised.append(dot3(pair[:, : 2 * RANK], wide(child[c * batch + u])))
        for u, up in enumerate(raised):
            nodes[leaves + c * batch + u, 0:16] = up
        return carry

    lax.fori_loop(0, parents // batch, moments, 0)

    root4 = jnp.zeros((16, LANES), F32)
    for g in range(parents // 4):
        left = jnp.zeros((16, LANES), F32)
        for q in range(4):
            left = jnp.where(group16 == q, nodes[leaves + 4 * g + q, 0:16], left)
        root4 = root4 + dot3(left, wide(root[g * LANES : (g + 1) * LANES]))

    for skeleton, first in ((leaf_skel, 0), (parent_skel, leaves)):
        pad_points[0:3, 0 : skeleton.shape[1]] = skeleton[...] - 1.5
        for g in range(skeleton.shape[1] // LANES):
            tile = pad_points[:, g * LANES : (g + 1) * LANES]
            for q in range(4):
                nodes[first + 4 * g + q, 16:24] = replicate_group(tile, group8, q)

    pad_points[:, 0:LANES] = jnp.zeros((8, LANES), F32)
    for row in range(3):
        pad_points[3:4, row * RANK : (row + 1) * RANK] = root_skel[row : row + 1, :] - 1.5
    width = top.shape[1]
    for row in range(2):
        start = 3 * RANK + row * width
        pad_points[3:4, start : start + width] = top[row : row + 1, :].astype(F32)
    lower_rows, _ = fold_maps()
    own = lax.broadcasted_iota(jnp.int32, (16, LANES), 0) % 4 == group16
    packed = pick(lower_rows, jnp.where(own, root4, 0.0))
    root_data = pad_points[:, 0:LANES] + packed

    group24 = lane_of((24, LANES)) // RANK
    row24 = lax.broadcasted_iota(jnp.int32, (24, LANES), 0)
    extra = jnp.concatenate([jnp.zeros((16, LANES), F32), root_data], axis=0)

    def pack(d, carry):
        block = jnp.zeros((24, LANES), F32)
        for q in range(4):
            send = leaf_send if q < 2 else parent_send
            node = send[q % 2, d]
            safe = jnp.maximum(node, 0) + (0 if q < 2 else leaves)
            block = jnp.where((group24 == q) & (node >= 0), nodes[safe], block)
        message[d] = jnp.where(row24 < 19, block, extra)
        return carry

    lax.fori_loop(0, peers, pack, 0, unroll=4)
    pl.semaphore_wait(barrier, peers - 1)

    def transfer(k):
        there = lax.rem(me + k, peers)
        return pltpu.make_async_remote_copy(
            src_ref=message.at[there],
            dst_ref=arrived.at[me],
            send_sem=send_sems.at[k],
            recv_sem=receive_sems.at[k],
            device_id={"leaf": there},
            device_id_type=pl.DeviceIdType.MESH,
        )

    def start(k, carry):
        transfer(k).start()
        return carry

    lax.fori_loop(1, peers, start, 0)
    arrived[me] = message[me]
    gather(point_table, 16, 8)

    def finish(k, carry):
        transfer(k).wait_send()
        come = lax.rem(me - k + peers, peers)
        pltpu.make_async_remote_copy(
            src_ref=message.at[come],
            dst_ref=arrived.at[come],
            send_sem=send_sems.at[k],
            recv_sem=receive_sems.at[k],
            device_id={"leaf": come},
            device_id_type=pl.DeviceIdType.MESH,
        ).wait_recv()
        return carry

    lax.fori_loop(1, peers, finish, 0)


def couple_kernel(
    used,
    near,
    leaf_pairs,
    parent_pairs,
    values,
    nodes,
    near_sum,
    far_sum,
    near_left,
    near_right,
    near_values,
    far_left,
    far_right,
    far_pieces,
):
    leaves = near_sum.shape[0]
    parents = leaves // 2
    near_sum[...] = jnp.zeros_like(near_sum)
    far_sum[...] = jnp.zeros_like(far_sum)
    lane16 = lane_of((16, LANES))
    group16 = lane16 // RANK
    group8 = lane_of((8, LANES)) // RANK
    lane32 = lane_of((32, LANES))
    group32 = lane32 // RANK
    lane64 = lane_of((64, LANES))

    def near_prep(g, carry):
        at = pl.ds(pl.multiple_of(g * LANES, LANES), LANES)
        target, source = features(values[16:24, at])
        turned = pltpu.roll(target, 64, 1)
        across = jnp.concatenate([source] * 4, axis=0).T
        tile = values[0:16, at]
        spun = pltpu.roll(tile, 64, 1)
        for j in range(2):
            low, high = (target, turned) if j == 0 else (turned, target)
            near_right[0, 2 * g + j] = jnp.where(lane32 < LEAF, low, 0.0).astype(BF16)
            near_right[1, 2 * g + j] = jnp.where(lane32 >= LEAF, high, 0.0).astype(BF16)
            part = across[64 * j : 64 * (j + 1)]
            near_left[0, 2 * g + j] = jnp.where(lane64 < RANK, part, 0.0).astype(BF16)[:, :64]
            near_left[1, 2 * g + j] = jnp.where(lane64 >= RANK, part, 0.0).astype(BF16)[:, :64]
            twice = jnp.where((lane16 < LEAF) == (j == 0), tile, spun)
            hi = twice.astype(BF16).astype(F32)
            both = jnp.where(lane16 < LEAF, hi, twice - hi).astype(BF16)
            near_values[2 * g + j] = jnp.concatenate([both, both], axis=1)
        return carry

    lax.fori_loop(0, parents, near_prep, 0, unroll=4)

    def far_prep(g, carry):
        tile = jnp.zeros((8, LANES), F32)
        for q in range(4):
            tile = jnp.where(group8 == q, nodes[4 * g + q, 16:24], tile)
        across = jnp.concatenate([features(tile)[1]] * 4, axis=0).T
        for j in range(4):
            n = 4 * g + j
            target = features(nodes[n, 16:24])[0]
            part = across[32 * j : 32 * (j + 1)]
            for q in range(4):
                far_right[q, n] = jnp.where(group32 == q, target, 0.0).astype(BF16)
                far_left[q, n] = jnp.where(group32 == q, part, 0.0).astype(BF16)
            m = nodes[n, 0:16]
            hi = m.astype(BF16).astype(F32)
            far_pieces[n] = jnp.where(group16 % 2 == 0, hi, m - hi).astype(BF16)
        return carry

    lax.fori_loop(0, (leaves + parents) // 4, far_prep, 0, unroll=2)

    def far(pairs, first):
        groups = pairs.shape[1] // 4
        unroll = 16 if groups % 16 == 0 else 1

        def body(c, carry):
            ids, fields = [], []
            for u in range(unroll):
                base = (c * unroll + u) * 4
                ts = [pairs[0, base + q] + first for q in range(4)]
                ss = [pairs[1, base + q] + first for q in range(4)]
                rhs = jnp.concatenate([far_right[q, ts[q]] for q in range(4)], axis=0)
                lhs = (far_left[0, ss[0]] + far_left[1, ss[1]]) + (
                    far_left[2, ss[2]] + far_left[3, ss[3]]
                )
                ids.append((ts, ss))
                fields.append(dot(lhs, rhs))
            fields = [split2(jnp.exp2(e)) for e in fields]
            gots = [
                dot(
                    jnp.concatenate([far_pieces[s] for s in ss], axis=0),
                    jnp.concatenate([hi, hi, lo, lo], axis=0),
                )
                for (ts, ss), (hi, lo) in zip(ids, fields)
            ]
            for (ts, ss), got in zip(ids, gots):
                for q in range(4):
                    part = got[16 * q : 16 * (q + 1)]
                    far_sum[ts[q]] += jnp.where(group16 == q, part, 0.0)
            return carry

        lax.fori_loop(0, groups // unroll, body, 0)

    far(leaf_pairs, 0)
    far(parent_pairs, leaves)

    near_width = near.shape[1]
    unroll = 24 if near_width % 48 == 0 else 1
    limit = used[0]

    def near_body(c, carry):
        fields, gots = [], []
        for u in range(unroll):
            base = (c * unroll + u) * 2
            rhs = jnp.concatenate(
                [near_right[0, near[0, base]], near_right[1, near[0, base + 1]]], axis=0
            )
            fields.append(dot(near_left[0, near[1, base]] + near_left[1, near[1, base + 1]], rhs))
        fields = [split2(jnp.exp2(e)) for e in fields]
        for u, (hi, lo) in enumerate(fields):
            base = (c * unroll + u) * 2
            lhs = jnp.concatenate(
                [near_values[near[1, base]], near_values[near[1, base + 1]]], axis=0
            )
            gots.append(dot(lhs, jnp.concatenate([hi, hi, lo, lo], axis=0)))
        for u, got in enumerate(gots):
            base = (c * unroll + u) * 2
            near_sum[near[0, base]] += jnp.where(
                (lane16 < LEAF) & (base < limit), got[:16], 0.0
            )
            near_sum[near[0, base + 1]] += jnp.where(
                (lane16 >= LEAF) & (base + 1 < limit), got[16:], 0.0
            )
        return carry

    chunk = 2 * unroll
    lax.fori_loop(0, (limit + chunk - 1) // chunk, near_body, 0)


def downward_kernel(
    peers,
    top_width,
    leaf_receive,
    parent_receive,
    arrived,
    nodes,
    order,
    basis,
    child,
    root,
    root_skel,
    near_sum,
    far_sum,
    product,
    pad_root,
    sorted_product,
    scattered,
):
    count = product.shape[1]
    tiles = count // LANES
    parents = child.shape[0]
    leaves = 2 * parents
    lane16 = lane_of((16, LANES))
    group16 = lane16 // RANK
    group8 = lane_of((8, LANES)) // RANK
    me = lax.axis_index("leaf")
    pad_root[...] = jnp.zeros_like(pad_root)
    pad_root[0:3, 0:RANK] = root_skel[...] - 1.5
    square = (LANES, LANES)
    diagonal = lax.broadcasted_iota(jnp.int32, square, 0) // RANK == lane_of(square) // RANK
    root_target = features(pad_root[...])[0].astype(BF16)
    top_targets = arrived[:, 19, :]
    top_sources = pltpu.roll(top_targets, LANES - top_width, 1)
    slot = lane_of(top_targets.shape) - 3 * RANK
    mine = (top_targets == me.astype(F32)) & (slot >= 0) & (slot < top_width)
    _, upper_rows = fold_maps()
    row8 = lax.broadcasted_iota(jnp.int32, (8, LANES), 0)
    own = lax.broadcasted_iota(jnp.int32, (16, LANES), 0) % 4 == group16

    def replicate(x):
        x = x + pltpu.roll(x, 64, 1)
        return x + pltpu.roll(x, 32, 1)

    def root_coords(block):
        line = jnp.where(row8 == 3, block, 0.0)
        spread = pltpu.roll(line, 5, 0) + pltpu.roll(line, 6, 0) + pltpu.roll(line, 7, 0)
        return replicate(jnp.where(row8 == group8, spread, 0.0))

    def root_moment(block):
        return replicate(jnp.where(own, pick(upper_rows, block), 0.0))
    batch = 8 if peers % 8 == 0 else 4

    def turn(source):
        return jnp.concatenate([source] * 4, axis=0).T.astype(BF16)[:, :RANK]

    def remote(c, field):
        all_targets, powers = [], []
        for u in range(batch):
            d = c * batch + u
            across = turn(features(arrived[d, 16:24])[1])
            coords = jnp.zeros((8, LANES), F32)
            targets = []
            for q in range(4):
                receive = leaf_receive if q < 2 else parent_receive
                node = receive[q % 2, d]
                safe = jnp.maximum(node, 0) + (0 if q < 2 else leaves)
                targets.append((safe, node >= 0))
                coords = jnp.where(group8 == q, nodes[safe, 16:24], coords)
            all_targets.append(targets)
            powers.append(dot(across, features(coords)[0].astype(BF16)))
        root_powers, root_moments = [], []
        for v in range(batch // 4):
            coords = jnp.zeros((8, LANES), F32)
            moments = jnp.zeros((16, LANES), F32)
            for q in range(4):
                d = c * batch + 4 * v + q
                weight = jnp.sum(
                    jnp.where(mine & (top_sources == d.astype(F32)), 1.0, 0.0), keepdims=True
                )
                block = arrived[d, 16:24]
                coords = jnp.where(group8 == q, root_coords(block), coords)
                moments = jnp.where(group16 == q, root_moment(block) * weight, moments)
            root_powers.append(dot(turn(features(coords)[1]), root_target))
            root_moments.append(moments)
        gots = [
            dot3(arrived[c * batch + u, 0:16], jnp.where(diagonal, jnp.exp2(e), 0.0))
            for u, e in enumerate(powers)
        ]
        for moments, e in zip(root_moments, root_powers):
            field = field + dot3(moments, jnp.exp2(e))
        for targets, got in zip(all_targets, gots):
            for q, (safe, live) in enumerate(targets):
                far_sum[safe] += jnp.where((group16 == q) & live, got, 0.0)
        return field

    field = lax.fori_loop(0, peers // batch, remote, jnp.zeros((16, LANES), F32))
    field = jnp.where(group16 == 0, field, 0.0)

    for g in range(parents // 4):
        got = dot3(field, wide(root[g * LANES : (g + 1) * LANES]), dot_nt)
        for q in range(4):
            far_sum[leaves + 4 * g + q] += jnp.where(group16 == q, got, 0.0)

    lower = 8

    def finish(c, carry):
        downs, boths = [], []
        for u in range(lower):
            m = c * lower + u
            block = wide(child[m])
            downs.append(
                dot3(far_sum[leaves + m], jnp.concatenate([block, block], axis=0), dot_nt)
            )
        for u, down in enumerate(downs):
            m = c * lower + u
            at = pl.ds(pl.multiple_of(m * LANES, LANES), LANES)
            first = far_sum[2 * m] + jnp.where(group16 == 0, down, 0.0)
            second = far_sum[2 * m + 1] + jnp.where(group16 == 1, down, 0.0)
            boths.append(
                dot3(
                    jnp.concatenate([first, second], axis=0),
                    jnp.concatenate([basis[:, at]] * 4, axis=0),
                )
            )
        for u, both in enumerate(boths):
            m = c * lower + u
            at = pl.ds(pl.multiple_of(m * LANES, LANES), LANES)
            x, y = near_sum[2 * m], near_sum[2 * m + 1]
            x = x + pltpu.roll(x, 64, 1) + both[:16]
            y = y + pltpu.roll(y, 64, 1) + both[16:]
            sorted_product[:, at] = jnp.where(lane16 < LEAF, x, y)
        return carry

    lax.fori_loop(0, parents // lower, finish, 0)

    step = 512
    scattered[...] = jnp.zeros_like(scattered)

    def scatter(t, carry):
        at = pl.ds(pl.multiple_of(t * step, step), step)
        where_to = order[:, at]
        hot = one_hot(where_to & (LANES - 1), step)
        high = where_to >> 7
        z = sorted_product[:, at]
        hi = z.astype(BF16).astype(F32)
        both = jnp.concatenate([hi, z - hi], axis=1)
        high2 = jnp.concatenate([high, high], axis=1)
        spread = jnp.concatenate(
            [jnp.where(high2 == h, both, 0.0).astype(BF16) for h in range(tiles)], axis=0
        )
        scattered[...] += dot_nt(spread, jnp.concatenate([hot, hot], axis=1))
        return carry

    lax.fori_loop(0, count // step, scatter, 0)
    for h in range(tiles):
        product[:, h * LANES : (h + 1) * LANES] = scattered[h * 16 : (h + 1) * 16]


def lower_kernel(peers, top_width, *refs):
    (used, near, leaf_pairs, parent_pairs, leaf_receive, parent_receive, arrived, values, nodes) = refs[:9]
    (order, basis, child, root, root_skel, product, near_sum, far_sum) = refs[9:17]
    tables, (pad_root, sorted_product, scattered) = refs[17:23], refs[23:]
    couple_kernel(used, near, leaf_pairs, parent_pairs, values, nodes, near_sum, far_sum, *tables)
    downward_kernel(
        peers,
        top_width,
        leaf_receive,
        parent_receive,
        arrived,
        nodes,
        order,
        basis,
        child,
        root,
        root_skel,
        near_sum,
        far_sum,
        product,
        pad_root,
        sorted_product,
        scattered,
    )


VM = pl.BlockSpec(memory_space=pltpu.VMEM)
SM = pl.BlockSpec(memory_space=pltpu.SMEM)
PARAMS = pltpu.CompilerParams(vmem_limit_bytes=28 * 1024 * 1024)


def shape(*dims, dtype=F32):
    return jax.ShapeDtypeStruct(dims, dtype)


def shards(
    right_sides,
    point_coords,
    cluster_order,
    leaf_basis,
    child_transfer,
    root_transfer,
    leaf_skeleton,
    parent_skeleton,
    root_skeleton,
    near_pairs,
    near_count,
    leaf_send,
    leaf_receive,
    parent_send,
    parent_receive,
    leaf_pairs,
    parent_pairs,
    top_pairs,
):
    peers = lax.axis_size("leaf")
    count = right_sides.shape[1]
    leaves = count // LEAF
    parents = leaves // 2
    both = leaves + parents
    order = cluster_order.reshape(1, count)
    child = child_transfer.reshape(parents, 2 * RANK, RANK)
    root = root_transfer.reshape(parents * RANK, RANK)

    def slots(plan):
        return plan.transpose(0, 2, 1).reshape(2, peers)

    values, nodes, arrived = pl.pallas_call(
        functools.partial(upward_kernel, peers),
        out_shape=(
            shape(24, count),
            shape(both, 24, LANES),
            shape(peers, ROWS, LANES),
        ),
        in_specs=[SM] * 2 + [VM] * 10,
        out_specs=(VM,) * 3,
        scratch_shapes=[
            pltpu.VMEM((8, count), F32),
            pltpu.VMEM((16 * (count // LANES), 2 * LANES), BF16),
            pltpu.VMEM((8 * (count // LANES), 2 * LANES), BF16),
            pltpu.VMEM((peers, ROWS, LANES), F32),
            pltpu.SemaphoreType.DMA((peers,)),
            pltpu.SemaphoreType.DMA((peers,)),
        ],
        compiler_params=pltpu.CompilerParams(
            vmem_limit_bytes=28 * 1024 * 1024, collective_id=0, has_side_effects=True
        ),
        name="upward",
    )(
        slots(leaf_send),
        slots(parent_send),
        right_sides,
        point_coords,
        order,
        leaf_basis,
        child,
        root,
        leaf_skeleton,
        parent_skeleton,
        root_skeleton,
        top_pairs,
    )
    return pl.pallas_call(
        functools.partial(lower_kernel, peers, top_pairs.shape[1]),
        out_shape=shape(16, count),
        in_specs=[SM] * 6 + [VM] * 8,
        out_specs=VM,
        scratch_shapes=[
            pltpu.VMEM((leaves, 16, LANES), F32),
            pltpu.VMEM((both, 16, LANES), F32),
            pltpu.VMEM((2, leaves, 64, 64), BF16),
            pltpu.VMEM((2, leaves, 32, LANES), BF16),
            pltpu.VMEM((leaves, 16, 256), BF16),
            pltpu.VMEM((4, both, 32, LANES), BF16),
            pltpu.VMEM((4, both, 32, LANES), BF16),
            pltpu.VMEM((both, 16, LANES), BF16),
            pltpu.VMEM((8, LANES), F32),
            pltpu.VMEM((16, count), F32),
            pltpu.VMEM((16 * (count // LANES), LANES), F32),
        ],
        compiler_params=PARAMS,
        name="lower",
    )(
        near_count,
        near_pairs,
        leaf_pairs,
        parent_pairs,
        slots(leaf_receive),
        slots(parent_receive),
        arrived,
        values,
        nodes,
        order,
        leaf_basis,
        child,
        root,
        root_skeleton,
    )


def solution(mesh):
    leaf = ("groups", "leaf")
    columns = P(None, leaf)
    nodes = P(leaf, None, None)
    in_specs = (
        columns,
        columns,
        P(leaf),
        columns,
        P(leaf, None),
        P(leaf, None),
        columns,
        columns,
        columns,
        columns,
        P(leaf),
        nodes,
        nodes,
        nodes,
        nodes,
        columns,
        columns,
        columns,
    )
    return jax.shard_map(
        shards, mesh=mesh, in_specs=in_specs, out_specs=columns, check_vma=False
    )
```

```python
import functools
import math

import jax
import jax.numpy as jnp
from jax import lax
from jax.experimental import pallas as pl
from jax.experimental.pallas import tpu as pltpu
from jax.sharding import PartitionSpec as P

LEAF = 64
RANK = 32
NRHS = 16
LANES = 128
ROWS = 24
SCALE = math.sqrt(math.log2(math.e))
F32 = jnp.float32
BF16 = jnp.bfloat16


def split2(x):
    hi = x.astype(BF16)
    return hi, (x - hi.astype(F32)).astype(BF16)


def dot(a, b):
    return jnp.dot(a, b, preferred_element_type=F32)


def dot_nt(a, b):
    return lax.dot_general(a, b, (((1,), (1,)), ((), ())), preferred_element_type=F32)


def dot3(a, b, product=dot):
    ah, al = split2(a)
    bh, bl = split2(b)
    return product(ah, bh) + (product(al, bh) + product(ah, bl))


def lane_of(shape):
    return lax.broadcasted_iota(jnp.int32, shape, len(shape) - 1)


def pieces3(x):
    one = x.astype(BF16).astype(F32)
    rest = x - one
    two = rest.astype(BF16).astype(F32)
    return one, two, rest - two


def features(coords):
    width = coords.shape[1]
    row = lax.broadcasted_iota(jnp.int32, (8, width), 0)
    a = jnp.where(row < 3, coords * SCALE, 0.0)
    norm = -0.5 * jnp.sum(a * a, axis=0, keepdims=True)
    a1, a2, a3 = pieces3(a)
    n1, n2, n3 = pieces3(norm)
    a4 = pltpu.roll(a2, 3, 0)
    up1 = pltpu.roll(a1, 3, 0)
    up3 = pltpu.roll(a3, 3, 0)
    one = jnp.ones((8, width), F32)
    zero = jnp.zeros((8, width), F32)

    def block(low, high, six, seven):
        return jnp.where(row < 3, low, jnp.where(row < 6, high, jnp.where(row == 6, six, seven)))

    target = (
        block(a1, up1, n1, n2),
        block(a2, a4, n3, one),
        block(a1, up3, one, one),
    )
    source = (
        block(a1, a4, one, one),
        block(a1, a4, one, n1),
        block(a3, up1, n2, n3),
    )
    return (
        jnp.concatenate(target + (zero,), axis=0),
        jnp.concatenate(source + (zero,), axis=0),
    )


def one_hot(low, width):
    return jnp.where(
        lax.broadcasted_iota(jnp.int32, (LANES, width), 0) == low, 1.0, 0.0
    ).astype(BF16)


def wide(block):
    return jnp.concatenate([block] * 4, axis=1)


def replicate_group(tile, group, which):
    kept = jnp.where(group == which, tile, 0.0)
    kept = kept + pltpu.roll(kept, 64, 1)
    return kept + pltpu.roll(kept, 32, 1)


def pick(chosen, x):
    return sum(dot(chosen, piece.astype(BF16)) for piece in pieces3(x))


def fold_maps():
    down = lax.broadcasted_iota(jnp.int32, (8, 16), 1) // 4 + 4
    down = down == lax.broadcasted_iota(jnp.int32, (8, 16), 0)
    back = lax.broadcasted_iota(jnp.int32, (16, 8), 0) // 4 + 4
    back = back == lax.broadcasted_iota(jnp.int32, (16, 8), 1)
    return (
        jnp.where(down, 1.0, 0.0).astype(BF16),
        jnp.where(back, 1.0, 0.0).astype(BF16),
    )


def upward_kernel(
    peers,
    leaf_send,
    parent_send,
    rhs,
    points,
    order,
    basis,
    child,
    root,
    leaf_skel,
    parent_skel,
    root_skel,
    top,
    values,
    nodes,
    arrived,
    pad_points,
    table,
    point_table,
    message,
    send_sems,
    receive_sems,
):
    me = lax.axis_index("leaf")
    barrier = pltpu.get_barrier_semaphore()

    def greet(k, carry):
        pl.semaphore_signal(
            barrier,
            inc=1,
            device_id={"leaf": lax.rem(me + k, peers)},
            device_id_type=pl.DeviceIdType.MESH,
        )
        return carry

    lax.fori_loop(1, peers, greet, 0)
    count = rhs.shape[1]
    tiles = count // LANES
    parents = child.shape[0]
    leaves = 2 * parents
    pad_points[...] = jnp.zeros_like(pad_points)
    pad_points[0:3, :] = points[...] - 1.5
    for h in range(tiles // 2):
        for source, rows, into in ((rhs, 32, table), (pad_points, 16, point_table)):
            both = jnp.concatenate(
                [
                    source[:, 2 * h * LANES : (2 * h + 1) * LANES],
                    source[:, (2 * h + 1) * LANES : (2 * h + 2) * LANES],
                ],
                axis=0,
            )
            hi, lo = split2(both)
            span = slice(h * rows, (h + 1) * rows)
            into[span, 0:LANES] = hi
            into[span, LANES : 2 * LANES] = lo

    step = 256

    def gather(source, first, rows):
        def body(t, carry):
            at = pl.ds(pl.multiple_of(t * step, step), step)
            where_from = order[:, at]
            high = where_from >> 7
            hot = one_hot(where_from & (LANES - 1), step)
            got = dot(source[...], jnp.concatenate([hot, hot], axis=0))
            total = jnp.zeros((rows, step), F32)
            for h in range(tiles):
                total = jnp.where(high == h, got[h * rows : (h + 1) * rows], total)
            values[first : first + rows, at] = total
            return carry

        lax.fori_loop(0, count // step, body, 0, unroll=2)

    gather(table, 0, 16)

    lane16 = lane_of((16, LANES))
    group16 = lane16 // RANK
    group8 = lane_of((8, LANES)) // RANK
    batch = 16 if parents % 16 == 0 else 1

    def moments(c, carry):
        found = []
        for u in range(batch):
            g = c * batch + u
            at = pl.ds(pl.multiple_of(g * LANES, LANES), LANES)
            vt = values[0:16, at]
            left = jnp.concatenate(
                [jnp.where(lane16 < LEAF, vt, 0.0), jnp.where(lane16 >= LEAF, vt, 0.0)], axis=0
            )
            found.append(dot3(left, jnp.concatenate([basis[:, at]] * 4, axis=0), dot_nt))
        for u, both in enumerate(found):
            g = c * batch + u
            nodes[2 * g, 0:16] = both[:16]
            nodes[2 * g + 1, 0:16] = both[16:]
        raised = []
        for u, both in enumerate(found):
            pair = jnp.where(lane16 < RANK, both[:16], both[16:])
            raised.append(dot3(pair[:, : 2 * RANK], wide(child[c * batch + u])))
        for u, up in enumerate(raised):
            nodes[leaves + c * batch + u, 0:16] = up
        return carry

    lax.fori_loop(0, parents // batch, moments, 0)

    root4 = jnp.zeros((16, LANES), F32)
    for g in range(parents // 4):
        left = jnp.zeros((16, LANES), F32)
        for q in range(4):
            left = jnp.where(group16 == q, nodes[leaves + 4 * g + q, 0:16], left)
        root4 = root4 + dot3(left, wide(root[g * LANES : (g + 1) * LANES]))

    for skeleton, first in ((leaf_skel, 0), (parent_skel, leaves)):
        pad_points[0:3, 0 : skeleton.shape[1]] = skeleton[...] - 1.5
        for g in range(skeleton.shape[1] // LANES):
            tile = pad_points[:, g * LANES : (g + 1) * LANES]
            for q in range(4):
                nodes[first + 4 * g + q, 16:24] = replicate_group(tile, group8, q)

    pad_points[:, 0:LANES] = jnp.zeros((8, LANES), F32)
    for row in range(3):
        pad_points[3:4, row * RANK : (row + 1) * RANK] = root_skel[row : row + 1, :] - 1.5
    width = top.shape[1]
    for row in range(2):
        start = 3 * RANK + row * width
        pad_points[3:4, start : start + width] = top[row : row + 1, :].astype(F32)
    lower_rows, _ = fold_maps()
    own = lax.broadcasted_iota(jnp.int32, (16, LANES), 0) % 4 == group16
    packed = pick(lower_rows, jnp.where(own, root4, 0.0))
    root_data = pad_points[:, 0:LANES] + packed

    group24 = lane_of((24, LANES)) // RANK
    row24 = lax.broadcasted_iota(jnp.int32, (24, LANES), 0)
    extra = jnp.concatenate([jnp.zeros((16, LANES), F32), root_data], axis=0)

    def pack(d, carry):
        block = jnp.zeros((24, LANES), F32)
        for q in range(4):
            send = leaf_send if q < 2 else parent_send
            node = send[q % 2, d]
            safe = jnp.maximum(node, 0) + (0 if q < 2 else leaves)
            block = jnp.where((group24 == q) & (node >= 0), nodes[safe], block)
        message[d] = jnp.where(row24 < 19, block, extra)
        return carry

    lax.fori_loop(0, peers, pack, 0, unroll=4)
    pl.semaphore_wait(barrier, peers - 1)

    def transfer(k):
        there = lax.rem(me + k, peers)
        return pltpu.make_async_remote_copy(
            src_ref=message.at[there],
            dst_ref=arrived.at[me],
            send_sem=send_sems.at[k],
            recv_sem=receive_sems.at[k],
            device_id={"leaf": there},
            device_id_type=pl.DeviceIdType.MESH,
        )

    def start(k, carry):
        transfer(k).start()
        return carry

    lax.fori_loop(1, peers, start, 0)
    arrived[me] = message[me]
    gather(point_table, 16, 8)

    def finish(k, carry):
        transfer(k).wait_send()
        come = lax.rem(me - k + peers, peers)
        pltpu.make_async_remote_copy(
            src_ref=message.at[come],
            dst_ref=arrived.at[come],
            send_sem=send_sems.at[k],
            recv_sem=receive_sems.at[k],
            device_id={"leaf": come},
            device_id_type=pl.DeviceIdType.MESH,
        ).wait_recv()
        return carry

    lax.fori_loop(1, peers, finish, 0)


def couple_kernel(
    used,
    near,
    leaf_pairs,
    parent_pairs,
    values,
    nodes,
    near_sum,
    far_sum,
    near_left,
    near_right,
    near_values,
    far_left,
    far_right,
    far_pieces,
):
    leaves = near_sum.shape[0]
    parents = leaves // 2
    near_sum[...] = jnp.zeros_like(near_sum)
    far_sum[...] = jnp.zeros_like(far_sum)
    lane16 = lane_of((16, LANES))
    group16 = lane16 // RANK
    group8 = lane_of((8, LANES)) // RANK
    lane32 = lane_of((32, LANES))
    group32 = lane32 // RANK
    lane64 = lane_of((64, LANES))

    def near_prep(g, carry):
        at = pl.ds(pl.multiple_of(g * LANES, LANES), LANES)
        target, source = features(values[16:24, at])
        turned = pltpu.roll(target, 64, 1)
        across = jnp.concatenate([source] * 4, axis=0).T
        tile = values[0:16, at]
        spun = pltpu.roll(tile, 64, 1)
        for j in range(2):
            low, high = (target, turned) if j == 0 else (turned, target)
            near_right[0, 2 * g + j] = jnp.where(lane32 < LEAF, low, 0.0).astype(BF16)
            near_right[1, 2 * g + j] = jnp.where(lane32 >= LEAF, high, 0.0).astype(BF16)
            part = across[64 * j : 64 * (j + 1)]
            near_left[0, 2 * g + j] = jnp.where(lane64 < RANK, part, 0.0).astype(BF16)[:, :64]
            near_left[1, 2 * g + j] = jnp.where(lane64 >= RANK, part, 0.0).astype(BF16)[:, :64]
            twice = jnp.where((lane16 < LEAF) == (j == 0), tile, spun)
            hi = twice.astype(BF16).astype(F32)
            both = jnp.where(lane16 < LEAF, hi, twice - hi).astype(BF16)
            near_values[2 * g + j] = jnp.concatenate([both, both], axis=1)
        return carry

    lax.fori_loop(0, parents, near_prep, 0, unroll=4)

    def far_prep(g, carry):
        tile = jnp.zeros((8, LANES), F32)
        for q in range(4):
            tile = jnp.where(group8 == q, nodes[4 * g + q, 16:24], tile)
        across = jnp.concatenate([features(tile)[1]] * 4, axis=0).T
        for j in range(4):
            n = 4 * g + j
            target = features(nodes[n, 16:24])[0]
            part = across[32 * j : 32 * (j + 1)]
            for q in range(4):
                far_right[q, n] = jnp.where(group32 == q, target, 0.0).astype(BF16)
                far_left[q, n] = jnp.where(group32 == q, part, 0.0).astype(BF16)
            m = nodes[n, 0:16]
            hi = m.astype(BF16).astype(F32)
            far_pieces[n] = jnp.where(group16 % 2 == 0, hi, m - hi).astype(BF16)
        return carry

    lax.fori_loop(0, (leaves + parents) // 4, far_prep, 0, unroll=2)

    def far(pairs, first):
        groups = pairs.shape[1] // 4
        unroll = 32 if groups % 32 == 0 else 1

        def body(c, carry):
            ids, fields = [], []
            for u in range(unroll):
                base = (c * unroll + u) * 4
                ts = [pairs[0, base + q] + first for q in range(4)]
                ss = [pairs[1, base + q] + first for q in range(4)]
                rhs = jnp.concatenate([far_right[q, ts[q]] for q in range(4)], axis=0)
                lhs = (far_left[0, ss[0]] + far_left[1, ss[1]]) + (
                    far_left[2, ss[2]] + far_left[3, ss[3]]
                )
                ids.append((ts, ss))
                fields.append(dot(lhs, rhs))
            fields = [split2(jnp.exp2(e)) for e in fields]
            gots = [
                dot(
                    jnp.concatenate([far_pieces[s] for s in ss], axis=0),
                    jnp.concatenate([hi, hi, lo, lo], axis=0),
                )
                for (ts, ss), (hi, lo) in zip(ids, fields)
            ]
            for (ts, ss), got in zip(ids, gots):
                for q in range(4):
                    part = got[16 * q : 16 * (q + 1)]
                    far_sum[ts[q]] += jnp.where(group16 == q, part, 0.0)
            return carry

        lax.fori_loop(0, groups // unroll, body, 0)

    far(leaf_pairs, 0)
    far(parent_pairs, leaves)

    near_width = near.shape[1]
    unroll = 24 if near_width % 48 == 0 else 1
    limit = used[0]

    def near_body(c, carry):
        fields, gots = [], []
        for u in range(unroll):
            base = (c * unroll + u) * 2
            rhs = jnp.concatenate(
                [near_right[0, near[0, base]], near_right[1, near[0, base + 1]]], axis=0
            )
            fields.append(dot(near_left[0, near[1, base]] + near_left[1, near[1, base + 1]], rhs))
        fields = [split2(jnp.exp2(e)) for e in fields]
        for u, (hi, lo) in enumerate(fields):
            base = (c * unroll + u) * 2
            lhs = jnp.concatenate(
                [near_values[near[1, base]], near_values[near[1, base + 1]]], axis=0
            )
            gots.append(dot(lhs, jnp.concatenate([hi, hi, lo, lo], axis=0)))
        for u, got in enumerate(gots):
            base = (c * unroll + u) * 2
            near_sum[near[0, base]] += jnp.where(
                (lane16 < LEAF) & (base < limit), got[:16], 0.0
            )
            near_sum[near[0, base + 1]] += jnp.where(
                (lane16 >= LEAF) & (base + 1 < limit), got[16:], 0.0
            )
        return carry

    chunk = 2 * unroll
    lax.fori_loop(0, (limit + chunk - 1) // chunk, near_body, 0)


def downward_kernel(
    peers,
    top_width,
    leaf_receive,
    parent_receive,
    arrived,
    nodes,
    order,
    basis,
    child,
    root,
    root_skel,
    near_sum,
    far_sum,
    product,
    pad_root,
    sorted_product,
    scattered,
):
    count = product.shape[1]
    tiles = count // LANES
    parents = child.shape[0]
    leaves = 2 * parents
    lane16 = lane_of((16, LANES))
    group16 = lane16 // RANK
    group8 = lane_of((8, LANES)) // RANK
    me = lax.axis_index("leaf")
    pad_root[...] = jnp.zeros_like(pad_root)
    pad_root[0:3, 0:RANK] = root_skel[...] - 1.5
    square = (LANES, LANES)
    diagonal = lax.broadcasted_iota(jnp.int32, square, 0) // RANK == lane_of(square) // RANK
    root_target = features(pad_root[...])[0].astype(BF16)
    top_targets = arrived[:, 19, :]
    top_sources = pltpu.roll(top_targets, LANES - top_width, 1)
    slot = lane_of(top_targets.shape) - 3 * RANK
    mine = (top_targets == me.astype(F32)) & (slot >= 0) & (slot < top_width)
    _, upper_rows = fold_maps()
    row8 = lax.broadcasted_iota(jnp.int32, (8, LANES), 0)
    own = lax.broadcasted_iota(jnp.int32, (16, LANES), 0) % 4 == group16

    def replicate(x):
        x = x + pltpu.roll(x, 64, 1)
        return x + pltpu.roll(x, 32, 1)

    def root_coords(block):
        line = jnp.where(row8 == 3, block, 0.0)
        spread = pltpu.roll(line, 5, 0) + pltpu.roll(line, 6, 0) + pltpu.roll(line, 7, 0)
        return replicate(jnp.where(row8 == group8, spread, 0.0))

    def root_moment(block):
        return replicate(jnp.where(own, pick(upper_rows, block), 0.0))
    batch = 8 if peers % 8 == 0 else 4

    def turn(source):
        return jnp.concatenate([source] * 4, axis=0).T.astype(BF16)[:, :RANK]

    def remote(c, field):
        all_targets, powers = [], []
        for u in range(batch):
            d = c * batch + u
            across = turn(features(arrived[d, 16:24])[1])
            coords = jnp.zeros((8, LANES), F32)
            targets = []
            for q in range(4):
                receive = leaf_receive if q < 2 else parent_receive
                node = receive[q % 2, d]
                safe = jnp.maximum(node, 0) + (0 if q < 2 else leaves)
                targets.append((safe, node >= 0))
                coords = jnp.where(group8 == q, nodes[safe, 16:24], coords)
            all_targets.append(targets)
            powers.append(dot(across, features(coords)[0].astype(BF16)))
        root_powers, root_moments = [], []
        for v in range(batch // 4):
            coords = jnp.zeros((8, LANES), F32)
            moments = jnp.zeros((16, LANES), F32)
            for q in range(4):
                d = c * batch + 4 * v + q
                weight = jnp.sum(
                    jnp.where(mine & (top_sources == d.astype(F32)), 1.0, 0.0), keepdims=True
                )
                block = arrived[d, 16:24]
                coords = jnp.where(group8 == q, root_coords(block), coords)
                moments = jnp.where(group16 == q, root_moment(block) * weight, moments)
            root_powers.append(dot(turn(features(coords)[1]), root_target))
            root_moments.append(moments)
        gots = [
            dot3(arrived[c * batch + u, 0:16], jnp.where(diagonal, jnp.exp2(e), 0.0))
            for u, e in enumerate(powers)
        ]
        for moments, e in zip(root_moments, root_powers):
            field = field + dot3(moments, jnp.exp2(e))
        for targets, got in zip(all_targets, gots):
            for q, (safe, live) in enumerate(targets):
                far_sum[safe] += jnp.where((group16 == q) & live, got, 0.0)
        return field

    field = lax.fori_loop(0, peers // batch, remote, jnp.zeros((16, LANES), F32))
    field = jnp.where(group16 == 0, field, 0.0)

    for g in range(parents // 4):
        got = dot3(field, wide(root[g * LANES : (g + 1) * LANES]), dot_nt)
        for q in range(4):
            far_sum[leaves + 4 * g + q] += jnp.where(group16 == q, got, 0.0)

    lower = 16 if parents % 16 == 0 else 1

    def finish(c, carry):
        downs, boths = [], []
        for u in range(lower):
            m = c * lower + u
            block = wide(child[m])
            downs.append(
                dot3(far_sum[leaves + m], jnp.concatenate([block, block], axis=0), dot_nt)
            )
        for u, down in enumerate(downs):
            m = c * lower + u
            at = pl.ds(pl.multiple_of(m * LANES, LANES), LANES)
            first = far_sum[2 * m] + jnp.where(group16 == 0, down, 0.0)
            second = far_sum[2 * m + 1] + jnp.where(group16 == 1, down, 0.0)
            boths.append(
                dot3(
                    jnp.concatenate([first, second], axis=0),
                    jnp.concatenate([basis[:, at]] * 4, axis=0),
                )
            )
        for u, both in enumerate(boths):
            m = c * lower + u
            at = pl.ds(pl.multiple_of(m * LANES, LANES), LANES)
            x, y = near_sum[2 * m], near_sum[2 * m + 1]
            x = x + pltpu.roll(x, 64, 1) + both[:16]
            y = y + pltpu.roll(y, 64, 1) + both[16:]
            sorted_product[:, at] = jnp.where(lane16 < LEAF, x, y)
        return carry

    lax.fori_loop(0, parents // lower, finish, 0)

    step = 512
    scattered[...] = jnp.zeros_like(scattered)

    def scatter(t, carry):
        at = pl.ds(pl.multiple_of(t * step, step), step)
        where_to = order[:, at]
        hot = one_hot(where_to & (LANES - 1), step)
        high = where_to >> 7
        z = sorted_product[:, at]
        hi = z.astype(BF16).astype(F32)
        both = jnp.concatenate([hi, z - hi], axis=1)
        high2 = jnp.concatenate([high, high], axis=1)
        spread = jnp.concatenate(
            [jnp.where(high2 == h, both, 0.0).astype(BF16) for h in range(tiles)], axis=0
        )
        scattered[...] += dot_nt(spread, jnp.concatenate([hot, hot], axis=1))
        return carry

    lax.fori_loop(0, count // step, scatter, 0, unroll=2)
    for h in range(tiles):
        product[:, h * LANES : (h + 1) * LANES] = scattered[h * 16 : (h + 1) * 16]


def lower_kernel(peers, top_width, *refs):
    (used, near, leaf_pairs, parent_pairs, leaf_receive, parent_receive, arrived, values, nodes) = refs[:9]
    (order, basis, child, root, root_skel, product, near_sum, far_sum) = refs[9:17]
    tables, (pad_root, sorted_product, scattered) = refs[17:23], refs[23:]
    couple_kernel(used, near, leaf_pairs, parent_pairs, values, nodes, near_sum, far_sum, *tables)
    downward_kernel(
        peers,
        top_width,
        leaf_receive,
        parent_receive,
        arrived,
        nodes,
        order,
        basis,
        child,
        root,
        root_skel,
        near_sum,
        far_sum,
        product,
        pad_root,
        sorted_product,
        scattered,
    )


VM = pl.BlockSpec(memory_space=pltpu.VMEM)
SM = pl.BlockSpec(memory_space=pltpu.SMEM)
PARAMS = pltpu.CompilerParams(vmem_limit_bytes=28 * 1024 * 1024)


def shape(*dims, dtype=F32):
    return jax.ShapeDtypeStruct(dims, dtype)


def shards(
    right_sides,
    point_coords,
    cluster_order,
    leaf_basis,
    child_transfer,
    root_transfer,
    leaf_skeleton,
    parent_skeleton,
    root_skeleton,
    near_pairs,
    near_count,
    leaf_send,
    leaf_receive,
    parent_send,
    parent_receive,
    leaf_pairs,
    parent_pairs,
    top_pairs,
):
    peers = lax.axis_size("leaf")
    count = right_sides.shape[1]
    leaves = count // LEAF
    parents = leaves // 2
    both = leaves + parents
    order = cluster_order.reshape(1, count)
    child = child_transfer.reshape(parents, 2 * RANK, RANK)
    root = root_transfer.reshape(parents * RANK, RANK)

    def slots(plan):
        return plan.transpose(0, 2, 1).reshape(2, peers)

    values, nodes, arrived = pl.pallas_call(
        functools.partial(upward_kernel, peers),
        out_shape=(
            shape(24, count),
            shape(both, 24, LANES),
            shape(peers, ROWS, LANES),
        ),
        in_specs=[SM] * 2 + [VM] * 10,
        out_specs=(VM,) * 3,
        scratch_shapes=[
            pltpu.VMEM((8, count), F32),
            pltpu.VMEM((16 * (count // LANES), 2 * LANES), BF16),
            pltpu.VMEM((8 * (count // LANES), 2 * LANES), BF16),
            pltpu.VMEM((peers, ROWS, LANES), F32),
            pltpu.SemaphoreType.DMA((peers,)),
            pltpu.SemaphoreType.DMA((peers,)),
        ],
        compiler_params=pltpu.CompilerParams(
            vmem_limit_bytes=28 * 1024 * 1024, collective_id=0, has_side_effects=True
        ),
        name="upward",
    )(
        slots(leaf_send),
        slots(parent_send),
        right_sides,
        point_coords,
        order,
        leaf_basis,
        child,
        root,
        leaf_skeleton,
        parent_skeleton,
        root_skeleton,
        top_pairs,
    )
    return pl.pallas_call(
        functools.partial(lower_kernel, peers, top_pairs.shape[1]),
        out_shape=shape(16, count),
        in_specs=[SM] * 6 + [VM] * 8,
        out_specs=VM,
        scratch_shapes=[
            pltpu.VMEM((leaves, 16, LANES), F32),
            pltpu.VMEM((both, 16, LANES), F32),
            pltpu.VMEM((2, leaves, 64, 64), BF16),
            pltpu.VMEM((2, leaves, 32, LANES), BF16),
            pltpu.VMEM((leaves, 16, 256), BF16),
            pltpu.VMEM((4, both, 32, LANES), BF16),
            pltpu.VMEM((4, both, 32, LANES), BF16),
            pltpu.VMEM((both, 16, LANES), BF16),
            pltpu.VMEM((8, LANES), F32),
            pltpu.VMEM((16, count), F32),
            pltpu.VMEM((16 * (count // LANES), LANES), F32),
        ],
        compiler_params=PARAMS,
        name="lower",
    )(
        near_count,
        near_pairs,
        leaf_pairs,
        parent_pairs,
        slots(leaf_receive),
        slots(parent_receive),
        arrived,
        values,
        nodes,
        order,
        leaf_basis,
        child,
        root,
        root_skeleton,
    )


def solution(mesh):
    leaf = ("groups", "leaf")
    columns = P(None, leaf)
    nodes = P(leaf, None, None)
    in_specs = (
        columns,
        columns,
        P(leaf),
        columns,
        P(leaf, None),
        P(leaf, None),
        columns,
        columns,
        columns,
        columns,
        P(leaf),
        nodes,
        nodes,
        nodes,
        nodes,
        columns,
        columns,
        columns,
    )
    return jax.shard_map(
        shards, mesh=mesh, in_specs=in_specs, out_specs=columns, check_vma=False
    )
```
